128 devices in a mesh: section: 4 (over z), tensor: 16 (over x_lo, y, core), dp: 2 (over x_hi).
Axes of the slice: x: 4 (x_hi: 2, x_lo: 2; x = x_hi * 2 + x_lo), y: 4, z: 4, core: 2. Of those that a mesh axis runs over, the one named last changes fastest.
Arguments:
- x_in: bfloat16 [4, 5376, 256], P('section', 'tensor', 'dp'), may hold values from -6 to 6
- final_hidden: bfloat16 [5376, 256], P('tensor', 'dp'), may hold values from -6.8 to 6.8
- w_up: bfloat16 [4, 5376, 21504], P('section', None, ('tensor', 'dp')), may hold values from -0.078125 to 0.078125
- w_down: bfloat16 [4, 21504, 5376], P('section', ('tensor', 'dp')), may hold values from -0.0390625 to 0.0390625
- table: bfloat16 [131072, 5376], P(('section', 'tensor', 'dp')), may hold values from -1.2274756 to 1.2274756
- token_ids: int32 [256], replicated, may hold values from 0 to 131071
- targets: int32 [256], replicated, may hold values from 0 to 131071
- proj_in: bfloat16 [4, 64, 21504], P('section', None, ('tensor', 'dp')), may hold values from -0.0390625 to 0.0390625
- proj_out: bfloat16 [4, 64, 5376], P('section'), may hold values from -1.5 to 1.5
- proj_vocab: bfloat16 [64, 131072], P(None, ('section', 'tensor', 'dp')), may hold values from -1.796875 to 1.796875
- proj_dim: bfloat16 [64, 5376], P(None, 'tensor'), may hold values from -0.078125 to 0.078125
Outputs:
- layer_grads: float32 [4, 2, 64, 64], P('section', 'dp')
- table_grads: float32 [2, 64, 64], P('dp')
The draws below stay inside these ranges and needn't reach their ends.
All inputs are finite; a program needn't handle non-finite values.
Results may differ from the reference program's by a relative error of at most 0.015.
Values may be sent and summed in bfloat16 or wider, within the bound.
A program may use at most 192 MiB of HBM per device.

```python
import math
import jax
import jax.numpy as jnp
import numpy as np
from jax import lax

D = 5376
FF = 21504
RANK = 64
SEQ_LEN = 128
SECTIONS = 4
TOKENS = 256
VOCAB = 131072


def shared_table(key, power):
    first = jax.random.fold_in(key, 0)
    base = jnp.clip(jax.random.normal(first, (VOCAB, D), jnp.float32), -4.9, 4.9)
    rising = (1.0 + 2.0 * jnp.arange(VOCAB, dtype=jnp.float32) / VOCAB) ** power
    values = base * (2.0 / math.sqrt(D)) * rising[:, None]
    return values


def draw_table(key, part):
    values = shared_table(key, 1.0)
    return values.astype(jnp.bfloat16)


def draw_final_hidden(key, part):
    key = jax.random.fold_in(key, 7)
    field = jnp.clip(jax.random.normal(key, (D, TOKENS), jnp.float32), -6.0, 6.0)
    return field.astype(jnp.bfloat16)


def place_ends(result, key, low, largest):
    index_at = [jax.random.randint(jax.random.fold_in(key, axis), (), 0, length) for axis, length in enumerate(result.shape)]
    longest = result.shape.index(max(result.shape))
    next_to = index_at[:longest] + [(index_at[longest] + 1) % result.shape[longest]] + index_at[longest + 1:]
    return result.at[tuple(index_at)].set(low).at[tuple(next_to)].set(largest)


def block_levels(key, dims, pieces, smallest, high):
    gain, own = 1.0, jax.random.fold_in(key, 6)
    for dim, parts in pieces:
        heights = jnp.exp(jax.random.uniform(jax.random.fold_in(own, dim), (parts,), jnp.float32, smallest / len(pieces), high / len(pieces)))
        gain = gain * jnp.repeat(heights, dims[dim] // parts).reshape([-1 if axis == dim else 1 for axis in range(len(dims))])
    return gain


def ranked_wide(own_key, extent, count, skew):
    loads = [min(1 << octave, count + 1 - (1 << octave)) * (1 << 20) // math.isqrt((1 << octave) ** skew) + 1 for octave in range((count + 1).bit_length()) if 1 << octave <= count]
    width = 1 + sum(loads) // (1 << 30)
    grid = np.cumsum(np.array([max(1, weight // width) for weight in loads]))
    pick = jax.random.randint(jax.random.fold_in(own_key, 1), extent, 0, int(grid[len(loads) - 1]))
    start = jnp.left_shift(1, jnp.searchsorted(jnp.asarray(grid, jnp.int32), pick, side="right").astype(jnp.int32))
    grade = start - 1 + jax.random.randint(jax.random.fold_in(own_key, 4), extent, 0, 1 << 30) % jnp.minimum(start, count + 1 - start)
    return jax.random.permutation(jax.random.fold_in(own_key, 2), count)[grade].astype(jnp.int32)


def bell_draw(rng, shape, deviation, bound, cuts=(), held_as=jnp.bfloat16):
    gain = block_levels(rng, shape, cuts, -0.22, 0.18) if cuts else 1.0
    entries = jax.random.normal(rng, shape, jnp.float32) * deviation * gain
    return jnp.minimum(jnp.maximum(entries, -bound), bound).astype(held_as)


def setup_inputs(seed: int = 0) -> dict:
    keys = jax.random.split(jax.random.key(seed), 12)
    x_in = bell_draw(keys[0], (SECTIONS, D, TOKENS), 1.0, 6.0, ((0, 4), (1, 16), (2, 2)))
    final_hidden = draw_final_hidden(jax.random.fold_in(keys[11], 71), 0)
    w_up = bell_draw(keys[2], (SECTIONS, D, FF), D ** -0.5, 0.078125, ((0, 4), (2, 32)))
    w_down = bell_draw(keys[3], (SECTIONS, FF, D), FF ** -0.5, 0.0390625, ((0, 4), (1, 32)))
    table = draw_table(jax.random.fold_in(keys[11], 71), 0)
    token_ids = place_ends(ranked_wide(keys[5], (TOKENS,), VOCAB, 2), jax.random.fold_in(keys[5], 3), 0, VOCAB - 1).astype(jnp.int32)
    targets = place_ends(ranked_wide(keys[6], (TOKENS,), VOCAB, 2), jax.random.fold_in(keys[6], 3), 0, VOCAB - 1).astype(jnp.int32)
    proj_in = bell_draw(keys[7], (SECTIONS, RANK, FF), FF ** -0.5, 0.0390625, ((0, 4), (2, 32)))
    proj_out = bell_draw(keys[8], (SECTIONS, RANK, D), 0.25, 1.5, ((0, 4),))
    proj_vocab = bell_draw(keys[9], (RANK, VOCAB), 0.3, 1.796875, ((1, 128),))
    proj_dim = bell_draw(keys[10], (RANK, D), D ** -0.5, 0.078125, ((1, 16),))
    return dict(x_in=x_in, final_hidden=final_hidden, w_up=w_up, w_down=w_down, table=table, token_ids=token_ids, targets=targets, proj_in=proj_in, proj_out=proj_out, proj_vocab=proj_vocab, proj_dim=proj_dim)


def silu_slope(hidden):
    gate = jax.nn.sigmoid(hidden)
    return gate * (1.0 + hidden * (1.0 - gate))

def per_sequence(left, right):
    count = left.shape[0] // SEQ_LEN
    return jnp.einsum('slr,slq->srq', left.reshape(count, SEQ_LEN, -1), right.reshape(count, SEQ_LEN, -1), precision=lax.Precision.HIGHEST)

def reference(x_in, final_hidden, w_up, w_down, table, token_ids, targets, proj_in, proj_out, proj_vocab, proj_dim):
    hidden_rows = final_hidden.T
    logits = jnp.dot(hidden_rows, table.T, preferred_element_type=jnp.float32)
    row_peak = lax.optimization_barrier(jnp.max(logits, axis=1, keepdims=True))
    exponent = jnp.exp(logits - row_peak)
    row_total = lax.optimization_barrier(jnp.sum(exponent, axis=1, keepdims=True))
    probability = exponent / row_total
    target_hot = (targets[:, None] == jnp.arange(VOCAB, dtype=jnp.int32)[None, :]).astype(jnp.float32)
    logit_grad = (probability - target_hot).astype(jnp.bfloat16)
    cotangent = jnp.dot(table.T, logit_grad.T, preferred_element_type=jnp.float32).astype(jnp.bfloat16)
    vocab_side = jnp.dot(logit_grad, proj_vocab.T, preferred_element_type=jnp.float32)
    dim_side = jnp.dot(hidden_rows, proj_dim.T, preferred_element_type=jnp.float32)
    token_side = jnp.take(proj_vocab, token_ids, axis=1).T.astype(jnp.float32)
    layer_list = []
    for layer_pos in reversed(range(SECTIONS)):
        hidden = jnp.dot(x_in[layer_pos].T, w_up[layer_pos], preferred_element_type=jnp.float32)
        activated = jax.nn.silu(hidden).astype(jnp.bfloat16)
        input_proj = jnp.dot(activated, proj_in[layer_pos].T, preferred_element_type=jnp.float32)
        output_proj = jnp.dot(cotangent.T, proj_out[layer_pos].T, preferred_element_type=jnp.float32)
        act_grad = jnp.dot(cotangent.T, w_down[layer_pos].T, preferred_element_type=jnp.float32)
        hidden_grad = (act_grad * silu_slope(hidden)).astype(jnp.bfloat16)
        backflow = jnp.dot(w_up[layer_pos], hidden_grad.T, preferred_element_type=jnp.float32)
        layer_list.append(per_sequence(output_proj, input_proj))
        cotangent = (cotangent.astype(jnp.float32) + backflow).astype(jnp.bfloat16)
    layer_grads = jnp.stack(layer_list[::-1], axis=0)
    embed_side = math.sqrt(D) * jnp.dot(cotangent.T, proj_dim.T, preferred_element_type=jnp.float32)
    table_grads = per_sequence(vocab_side, dim_side) + per_sequence(token_side, embed_side)
    return (layer_grads, table_grads)
```

```python
import math

import jax
import jax.numpy as jnp
from jax import lax
from jax.experimental import pallas as pl
from jax.experimental.pallas import tpu as pltpu
from jax.sharding import PartitionSpec as P

D = 5376
TOK = 256
SEQ = 128
RANK = 64
UNITS = 672
VROWS = 1024
ROWS = 336
KB = 768
NB = D // KB
PAD = 768
BF = jnp.bfloat16
F32 = jnp.float32


def dot(a, b, dims=((1,), (0,)), precision=None):
    return lax.dot_general(a, b, (dims, ((), ())), preferred_element_type=F32, precision=precision)


def outer_pair(left, right):
    parts = [
        dot(left[:, q * SEQ:(q + 1) * SEQ], right[:, q * SEQ:(q + 1) * SEQ], ((1,), (1,)), lax.Precision.HIGHEST)
        for q in range(2)
    ]
    return jnp.concatenate(parts, axis=1)


def kernel(
    x_hbm, fh_hbm, wup_hbm, wdn_hbm, tab_hbm, tok, tgt, pin, pout, pvoc, pdim,
    lay_out, tab_out,
    tab, wup, wdn, fh, xb, cot,
    ph, pc, r0, r1, r2, s1, q0, q1, q2, u1, zr,
    logits, gradt, hid, slope, hgrad, inproj, vside, own,
    sm_cur, sm_slot, st_cur, st_slot, la_cur, la_slot, ta_cur, ta_slot,
    lsem, ag_send, ag_recv, rs_send, rs_recv, z_send, z_recv, c_send, c_recv, ar_send, ar_recv,
):
    sec = lax.axis_index("section")
    ten = lax.axis_index("tensor")
    dp = lax.axis_index("dp")
    c = ten % 2
    y = (ten // 2) % 4
    x = dp * 2 + ten // 8

    def dev(xx, yy, cc, zz):
        return (zz, (xx % 2) * 8 + yy * 2 + cc, xx // 2)

    def at(ka, kb):
        return (x + ka * (1 - c) + kb * c) % 4, (y + ka * c + kb * (1 - c)) % 4

    def cidx(xx, yy, cc):
        return xx * 8 + yy * 2 + cc

    def piece(ref, i):
        return ref.at[pl.ds(pl.multiple_of(i * ROWS, 16), ROWS)]

    def rows(i):
        return pl.ds(pl.multiple_of(i * ROWS, 16), ROWS)

    def rc(src, dst, ssem, rsem, device):
        return pltpu.make_async_remote_copy(
            src_ref=src, dst_ref=dst, send_sem=ssem, recv_sem=rsem,
            device_id=device, device_id_type=pl.DeviceIdType.MESH,
        )

    sib = dev(x, y, 1 - c, sec)
    mine = cidx(x, y, c)

    local = [
        pltpu.make_async_copy(fh_hbm, piece(fh, mine), lsem.at[0]),
        pltpu.make_async_copy(x_hbm, piece(xb, mine), lsem.at[1]),
        pltpu.make_async_copy(tab_hbm, tab, lsem.at[2]),
        pltpu.make_async_copy(wup_hbm, wup, lsem.at[3]),
        pltpu.make_async_copy(wdn_hbm, wdn, lsem.at[4]),
    ]
    for copy in local:
        copy.start()

    barrier = pltpu.get_barrier_semaphore()
    partners = [sib]
    for k in range(1, 4):
        partners.append(dev((x + k) % 4, y, c, sec))
        partners.append(dev(x, (y + k) % 4, c, sec))
        partners.append(dev(x, y, c, (sec + k) % 4))
    for partner in partners:
        pl.semaphore_signal(barrier, inc=1, device_id=partner, device_id_type=pl.DeviceIdType.MESH)
    pl.semaphore_wait(barrier, len(partners))

    def ag_copy(n, buf, i, device):
        return rc(piece(buf, i), piece(buf, i), ag_send.at[n], ag_recv.at[n, i], device)

    def ag_first(n, buf):
        for k in range(1, 4):
            xx, yy = at(k, 0)
            ag_copy(n, buf, mine, dev(xx, yy, c, sec)).start()
        ag_copy(n, buf, mine, sib).start()

    def ag_second(n, buf):
        for ka in range(4):
            xx, yy = at(4 - ka, 0)
            i = cidx(xx, yy, c)
            if ka:
                ag_copy(n, buf, i, sib).wait_recv()
            for kb in range(1, 4):
                xx, yy = at(0, kb)
                ag_copy(n, buf, i, dev(xx, yy, c, sec)).start()
            if ka:
                ag_copy(n, buf, i, sib).start()

    def ag_third(n, buf):
        def body(j, carry):
            xx, yy = at(4 - j % 4, 3 - j // 4)
            i = cidx(xx, yy, c)
            ag_copy(n, buf, i, sib).wait_recv()
            ag_copy(n, buf, i, sib).start()
            return carry

        lax.fori_loop(0, 12, body, 0)

    def ag_last(n, buf):
        def body(j, carry):
            ag_copy(n, buf, cidx(j // 4, j % 4, 1 - c), sib).wait_recv()
            return carry

        lax.fori_loop(0, 16, body, 0)

    def ag_drain(n, buf):
        part = buf.at[pl.ds(0, 31 * ROWS)]
        rc(part, part, ag_send.at[n], ag_recv.at[n, 0], sib).wait_send()

    def rs(n, src, pair, store, b0, b1, b2, held):
        def to_sibling(j, carry):
            t = 2 * j + 1 - c
            if store:
                for r, value in enumerate(pair(t)):
                    src[rows(r * 16 + t), :] = value.astype(BF)
            for r in range(2):
                slot = r * 8 + j
                rc(piece(src, r * 16 + t), piece(b0, slot), rs_send.at[n], rs_recv.at[n, slot], sib).start()
            return carry

        lax.fori_loop(0, 8, to_sibling, 0)
        first = x * (1 - c) + y * c

        def to_first(j, carry):
            t = 2 * j + c
            values = pair(t)
            for r in range(2):
                slot = r * 8 + j
                xx = r * 2 + j // 4
                yy = j % 4
                rc(piece(b0, slot), piece(b0, slot), rs_send.at[n], rs_recv.at[n, slot], sib).wait_recv()
                src[rows(r * 16 + t), :] = (values[r] + b0[rows(slot), :].astype(F32)).astype(BF)
                aa = xx * (1 - c) + yy * c
                bb = yy * (1 - c) + xx * c
                k = (aa - first + 4) % 4

                @pl.when(k != 0)
                def _():
                    px, py = at(k, 0)
                    spot = (k - 1) * 4 + bb
                    rc(
                        piece(src, r * 16 + t), piece(b1, spot), rs_send.at[n], rs_recv.at[n, 16 + spot],
                        dev(px, py, c, sec),
                    ).start()

            return carry

        lax.fori_loop(0, 8, to_first, 0)
        second = y * (1 - c) + x * c
        for kb in (1, 2, 3, 0):
            xx, yy = at(0, kb)
            bb = (second + kb) % 4
            total = src[rows(cidx(xx, yy, c)), :].astype(F32)
            for k in range(3):
                spot = k * 4 + bb
                rc(piece(b1, spot), piece(b1, spot), rs_send.at[n], rs_recv.at[n, 16 + spot], sib).wait_recv()
                total = total + b1[rows(spot), :].astype(F32)
            if kb:
                held[rows(kb - 1), :] = total.astype(BF)
                rc(
                    piece(held, kb - 1), piece(b2, kb - 1), rs_send.at[n], rs_recv.at[n, 27 + kb],
                    dev(xx, yy, c, sec),
                ).start()
        for k in range(3):
            rc(piece(b2, k), piece(b2, k), rs_send.at[n], rs_recv.at[n, 28 + k], sib).wait_recv()
            total = total + b2[rows(k), :].astype(F32)
        return total

    def rs_drain(n, src):
        part = src.at[pl.ds(0, 31 * ROWS)]
        rc(part, part, rs_send.at[n], rs_recv.at[n, 0], sib).wait_send()

    def ar_peers(phase):
        if phase == 0:
            return [(0, sib)]
        if phase == 1:
            return [(k, dev((x + k) % 4, y, c, sec)) for k in (1, 2, 3)]
        if phase == 2:
            return [(3 + k, dev(x, (y + k) % 4, c, sec)) for k in (1, 2, 3)]
        return [(6 + k, dev(x, y, c, (sec + k) % 4)) for k in (1, 2, 3)]

    def ar_copies(n, cur, slot, phase):
        return [
            rc(cur.at[phase], slot.at[s], ar_send.at[n], ar_recv.at[n, s], device)
            for s, device in ar_peers(phase)
        ]

    def ar_start(n, cur, slot, phase):
        for copy in ar_copies(n, cur, slot, phase):
            copy.start()

    def ar_wait(n, cur, slot, phase):
        for copy in ar_copies(n, cur, slot, phase):
            copy.wait_recv()

    def ar_sum(n, cur, slot, phase):
        ar_wait(n, cur, slot, phase)
        total = cur[phase].astype(F32)
        for s, _ in ar_peers(phase):
            total = total + slot[s].astype(F32)
        cur[phase + 1] = total.astype(cur.dtype)

    def ar_drain(n, slot, count):
        part = slot.at[pl.ds(0, count)]
        rc(part, part, ar_send.at[n], ar_recv.at[n, 0], sib).wait_send()

    local[0].wait()
    ag_first(0, fh)
    local[1].wait()

    columns = ((sec * 16 + ten) * 2 + dp) * VROWS + lax.broadcasted_iota(jnp.int32, (VROWS, TOK), 0)
    dim_part = dot(pdim[...], fh[rows(mine), :])
    dim_part = jnp.where(sec == 0, dim_part, jnp.zeros_like(dim_part))
    blank = jnp.zeros_like(dim_part)
    sm_cur[0, 0:RANK, 0:SEQ] = jnp.where(dp == 0, dim_part, blank).astype(BF)
    sm_cur[0, 0:RANK, SEQ:TOK] = jnp.where(dp == 1, dim_part, blank).astype(BF)
    token_hot = jnp.where(tok[...] == columns, 1.0, 0.0).astype(BF)
    sm_cur[0, RANK:2 * RANK, :] = dot(pvoc[...], token_hot).astype(BF)

    ag_second(0, fh)
    ar_start(0, sm_cur, sm_slot, 0)
    ag_third(0, fh)
    ag_first(1, xb)
    ag_last(0, fh)

    local[2].wait()
    logits[...] = jnp.zeros_like(logits)

    def logit_step(b, carry):
        k0 = pl.multiple_of(b * KB, KB)
        k1 = pl.multiple_of(D + b * KB, KB)
        right = jnp.concatenate([fh[pl.ds(k0, KB), :], fh[pl.ds(k1, KB), :]], axis=1)
        logits[...] += dot(tab[:, pl.ds(k0, KB)], right)
        return carry

    lax.fori_loop(0, NB, logit_step, 0)
    ag_second(1, xb)
    ar_sum(0, sm_cur, sm_slot, 0)
    ar_start(0, sm_cur, sm_slot, 1)

    peak = jnp.max(logits[...], axis=0, keepdims=True)
    st_cur[0] = jnp.zeros((8, TOK), F32)
    st_cur[0, 0:1, :] = peak
    st_cur[0, 1:2, :] = jnp.sum(jnp.exp(logits[...] - peak), axis=0, keepdims=True)
    ar_start(1, st_cur, st_slot, 0)
    ag_third(1, xb)

    def stats_step(phase):
        ar_wait(1, st_cur, st_slot, phase)
        peaks = [st_cur[phase, 0:1, :]] + [st_slot[s, 0:1, :] for s, _ in ar_peers(phase)]
        sums = [st_cur[phase, 1:2, :]] + [st_slot[s, 1:2, :] for s, _ in ar_peers(phase)]
        top = peaks[0]
        for other in peaks[1:]:
            top = jnp.maximum(top, other)
        total = jnp.zeros_like(top)
        for a, b in zip(peaks, sums):
            total = total + b * jnp.exp(a - top)
        st_cur[phase + 1] = jnp.zeros((8, TOK), F32)
        st_cur[phase + 1, 0:1, :] = top
        st_cur[phase + 1, 1:2, :] = total
        if phase < 3:
            ar_start(1, st_cur, st_slot, phase + 1)

    stats_step(0)
    local[3].wait()
    ag_last(1, xb)
    stats_step(1)

    hid[...] = jnp.zeros_like(hid)

    def hidden_step(b, carry):
        k0 = pl.multiple_of(b * KB, KB)
        k1 = pl.multiple_of(D + b * KB, KB)
        left = jnp.concatenate([xb[pl.ds(k0, KB), :], xb[pl.ds(k1, KB), :]], axis=1)
        hid[:, 0:UNITS] += dot(left.T, wup[pl.ds(k0, KB), :])
        return carry

    lax.fori_loop(0, 4, hidden_step, 0)
    stats_step(2)
    lax.fori_loop(4, NB, hidden_step, 0)
    stats_step(3)

    top = st_cur[4, 0:1, :]
    scale = 1.0 / st_cur[4, 1:2, :]
    hot = jnp.where(tgt[...] == columns, 1.0, 0.0)
    grad = jnp.exp(logits[...] - top) * scale - hot
    logits[...] = grad
    gradt[...] = grad.T.astype(BF)

    def head_step(b, carry):
        k0 = pl.multiple_of(b * KB, KB)
        k1 = pl.multiple_of(D + b * KB, KB)
        block = dot(gradt[...], tab[:, pl.ds(k0, KB)]).T.astype(BF)
        ph[pl.ds(k0, KB), :] = block[:, 0:SEQ]
        ph[pl.ds(k1, KB), :] = block[:, SEQ:TOK]
        return carry

    lax.fori_loop(0, NB, head_step, 0)

    def head_pair(t):
        return ph[rows(t), :].astype(F32), ph[rows(16 + t), :].astype(F32)

    ar_sum(0, sm_cur, sm_slot, 1)
    ar_start(0, sm_cur, sm_slot, 2)
    own[...] = rs(0, ph, head_pair, False, r0, r1, r2, s1)

    @pl.when(sec != 3)
    def _():
        zr[rows(3), :] = own[...].astype(BF)
        rc(piece(zr, 3), piece(zr, sec), z_send, z_recv.at[sec], dev(x, y, c, 3)).start()

    hidden = hid[...].T[0:UNITS, :]
    gate = jax.nn.sigmoid(hidden)
    slope[...] = gate * (1.0 + hidden * (1.0 - gate))
    inproj[...] = dot(pin[...], (hidden * gate).astype(BF))
    vside[...] = dot(pvoc[...], logits[...].astype(BF))
    local[4].wait()

    ar_sum(0, sm_cur, sm_slot, 2)
    ar_start(0, sm_cur, sm_slot, 3)

    @pl.when(sec == 3)
    def _():
        total = own[...]
        for s in range(3):
            rc(piece(zr, s), piece(zr, s), z_send, z_recv.at[s], sib).wait_recv()
            total = total + zr[rows(s), :].astype(F32)
        cot[rows(mine), :] = total.astype(BF)

    @pl.when(sec != 3)
    def _():
        rc(piece(cot, mine), piece(cot, mine), c_send, c_recv, sib).wait_recv()

    ag_first(2, cot)
    ag_second(2, cot)
    ag_third(2, cot)
    ag_last(2, cot)
    hid_rows = hgrad
    act = jnp.zeros((UNITS, TOK), F32)

    def down_step(b, acc):
        k0 = pl.multiple_of(b * KB, KB)
        k1 = pl.multiple_of(D + b * KB, KB)
        right = jnp.concatenate([cot[pl.ds(k0, KB), :], cot[pl.ds(k1, KB), :]], axis=1)
        return acc + dot(wdn[:, pl.ds(k0, KB)], right)

    act = lax.fori_loop(0, NB, down_step, act)
    hid_rows[...] = (act * slope[...]).astype(BF)

    def back_pair(t):
        block = dot(wup[rows(t), :], hgrad[...])
        return block[:, 0:SEQ], block[:, SEQ:TOK]

    back = rs(1, pc, back_pair, True, q0, q1, q2, u1)
    own[...] = (back + cot[rows(mine), :].astype(F32)).astype(BF).astype(F32)

    @pl.when(sec != 0)
    def _():
        zr[rows(4), :] = own[...].astype(BF)
        rc(piece(zr, 4), piece(cot, mine), c_send, c_recv, dev(x, y, c, (sec + 3) % 4)).start()

    def out_step(b, acc):
        k0 = pl.multiple_of(b * KB, KB)
        k1 = pl.multiple_of(D + b * KB, KB)
        right = jnp.concatenate([cot[pl.ds(k0, KB), :], cot[pl.ds(k1, KB), :]], axis=1)
        return acc + dot(pout[:, pl.ds(k0, KB)], right)

    outproj = lax.fori_loop(0, NB, out_step, jnp.zeros((RANK, TOK), F32))
    la_cur[0] = outer_pair(outproj, inproj[...])
    ar_start(2, la_cur, la_slot, 0)
    ar_sum(0, sm_cur, sm_slot, 3)
    ta_cur[0] = outer_pair(vside[...], sm_cur[4, 0:RANK, :].astype(F32))

    @pl.when(sec == 0)
    def _():
        embed = math.sqrt(D) * dot(pdim[...], own[...].astype(BF))
        first = jnp.where(dp == 0, embed, jnp.zeros_like(embed))
        second = jnp.where(dp == 1, embed, jnp.zeros_like(embed))
        both = jnp.concatenate([first, second], axis=1)
        ta_cur[0] += outer_pair(sm_cur[4, RANK:2 * RANK, :].astype(F32), both)

    ar_start(3, ta_cur, ta_slot, 0)
    for phase in range(3):
        ar_sum(2, la_cur, la_slot, phase)
        if phase < 2:
            ar_start(2, la_cur, la_slot, phase + 1)
        ar_sum(3, ta_cur, ta_slot, phase)
        ar_start(3, ta_cur, ta_slot, phase + 1)
    lay_out[...] = jnp.where(dp == 0, la_cur[3, :, 0:RANK], la_cur[3, :, RANK:2 * RANK])
    ar_sum(3, ta_cur, ta_slot, 3)
    tab_out[...] = jnp.where(dp == 0, ta_cur[4, :, 0:RANK], ta_cur[4, :, RANK:2 * RANK])

    ag_drain(0, fh)
    ag_drain(1, xb)
    ag_drain(2, cot)
    rs_drain(0, ph)
    rs_drain(1, pc)
    ar_drain(0, sm_slot, 10)
    ar_drain(1, st_slot, 10)
    ar_drain(2, la_slot, 7)
    ar_drain(3, ta_slot, 10)

    @pl.when(sec != 3)
    def _():
        rc(piece(zr, 3), piece(zr, 3), z_send, z_recv.at[0], sib).wait_send()

    @pl.when(sec != 0)
    def _():
        rc(piece(zr, 4), piece(zr, 4), c_send, c_recv, sib).wait_send()


def shards(x_in, final_hidden, w_up, w_down, table, token_ids, targets, proj_in, proj_out, proj_vocab, proj_dim):
    vmem = pl.BlockSpec(memory_space=pltpu.VMEM)
    hbm = pl.BlockSpec(memory_space=pl.ANY)
    full = lambda n: pltpu.VMEM((n * ROWS, SEQ), BF)
    dma = pltpu.SemaphoreType.DMA
    layer, tab = pl.pallas_call(
        kernel,
        out_shape=[jax.ShapeDtypeStruct((RANK, RANK), F32)] * 2,
        in_specs=[hbm] * 5 + [vmem] * 6,
        out_specs=[vmem] * 2,
        scratch_shapes=[
            pltpu.VMEM((VROWS, D), BF),
            pltpu.VMEM((D, UNITS), BF),
            pltpu.VMEM((UNITS, D), BF),
            full(32), full(32), full(32),
            full(32), full(32),
            full(16), full(12), full(3), full(3),
            full(16), full(12), full(3), full(3),
            full(5),
            pltpu.VMEM((VROWS, TOK), F32),
            pltpu.VMEM((TOK, VROWS), BF),
            pltpu.VMEM((TOK, PAD), F32),
            pltpu.VMEM((UNITS, TOK), F32),
            pltpu.VMEM((UNITS, TOK), BF),
            pltpu.VMEM((RANK, TOK), F32),
            pltpu.VMEM((RANK, TOK), F32),
            pltpu.VMEM((ROWS, SEQ), F32),
            pltpu.VMEM((5, 2 * RANK, TOK), BF),
            pltpu.VMEM((10, 2 * RANK, TOK), BF),
            pltpu.VMEM((5, 8, TOK), F32),
            pltpu.VMEM((10, 8, TOK), F32),
            pltpu.VMEM((5, RANK, 2 * RANK), F32),
            pltpu.VMEM((10, RANK, 2 * RANK), F32),
            pltpu.VMEM((5, RANK, 2 * RANK), F32),
            pltpu.VMEM((10, RANK, 2 * RANK), F32),
            dma((5,)),
            dma((3,)), dma((3, 32)),
            dma((2,)), dma((2, 31)),
            dma(()), dma((3,)),
            dma(()), dma(()),
            dma((4,)), dma((4, 10)),
        ],
        compiler_params=pltpu.CompilerParams(
            collective_id=0, has_side_effects=True, vmem_limit_bytes=62 * 1024 * 1024
        ),
    )(
        x_in[0], final_hidden, w_up[0], w_down[0], table,
        token_ids.reshape(1, TOK), targets.reshape(1, TOK),
        proj_in[0], proj_out[0], proj_vocab, proj_dim,
    )
    return layer[None, None], tab[None]


def solution(mesh):
    placed = (
        P("section", "tensor", "dp"),
        P("tensor", "dp"),
        P("section", None, ("tensor", "dp")),
        P("section", ("tensor", "dp"), None),
        P(("section", "tensor", "dp"), None),
        P(),
        P(),
        P("section", None, ("tensor", "dp")),
        P("section", None, None),
        P(None, ("section", "tensor", "dp")),
        P(None, "tensor"),
    )
    return jax.shard_map(
        shards,
        mesh=mesh,
        in_specs=placed,
        out_specs=(P("section", "dp", None, None), P("dp", None, None)),
        check_vma=False,
    )
```

```python
import math

import jax
import jax.numpy as jnp
from jax import lax
from jax.experimental import pallas as pl
from jax.experimental.pallas import tpu as pltpu
from jax.sharding import PartitionSpec as P

D = 5376
TOK = 256
SEQ = 128
RANK = 64
UNITS = 672
VROWS = 1024
ROWS = 336
PARTS = 3
SUB = ROWS // PARTS
PART = D // PARTS
HALF = D // 2
TB = 384
HB = 896
BF = jnp.bfloat16
F32 = jnp.float32


def dot(a, b, dims=((1,), (0,)), precision=None):
    return lax.dot_general(a, b, (dims, ((), ())), preferred_element_type=F32, precision=precision)


def outer_pair(left, right):
    parts = [
        dot(left[:, q * SEQ:(q + 1) * SEQ], right[:, q * SEQ:(q + 1) * SEQ], ((1,), (1,)), lax.Precision.HIGHEST)
        for q in range(2)
    ]
    return jnp.concatenate(parts, axis=1)


def kernel(
    x_hbm, fh_hbm, wupt_hbm, wdn_hbm, tab_hbm, tok, tgt, pin, pout, pvoc, pdim,
    lay_out, tab_out,
    tab, wupt, wup, wdn, fh, xb, cot, pdt,
    r0, r1, r2, zr,
    logits, gradt, act, slope, hgrad, inproj, vside, upside, own, sums,
    sm_cur, sm_slot, st_cur, st_slot, la_cur, la_slot, ta_cur, ta_slot,
    lsem, ag_send, ag_recv, rs_send, rs_recv, z_send, z_recv, c_send, c_recv, ar_send, ar_recv,
):
    sec = lax.axis_index("section")
    ten = lax.axis_index("tensor")
    dp = lax.axis_index("dp")
    c = ten % 2
    y = (ten // 2) % 4
    lo = ten // 8
    x = dp * 2 + lo

    def dev(xx, yy, cc, zz):
        return (zz, (xx % 2) * 8 + yy * 2 + cc, xx // 2)

    def at(ka, kb):
        return (x + ka * (1 - c) + kb * c) % 4, (y + ka * c + kb * (1 - c)) % 4

    def cidx(xx, yy, cc):
        return xx * 8 + yy * 2 + cc

    def rows(i):
        return pl.ds(pl.multiple_of(i * ROWS, 16), ROWS)

    def piece(ref, i):
        return ref.at[rows(i)]

    def span(start, count):
        return pl.ds(pl.multiple_of(start, 16), count)

    def given(xx, yy, cc, s):
        return span((xx * 8 + yy * 2 + cc) * ROWS + s * SUB, SUB)

    def chain_start(xx, yy, cc, s):
        spot = (1 - cc) * ((xx % 2) * 4 + yy) + cc * (yy * 2 + xx % 2)
        return (xx // 2) * D + s * PART + (cc * 8 + spot) * SUB

    def chained(xx, yy, cc, s):
        return span(chain_start(xx, yy, cc, s), SUB)

    def rc(src, dst, ssem, rsem, device):
        return pltpu.make_async_remote_copy(
            src_ref=src, dst_ref=dst, send_sem=ssem, recv_sem=rsem,
            device_id=device, device_id_type=pl.DeviceIdType.MESH,
        )

    sib = dev(x, y, 1 - c, sec)
    mine = cidx(x, y, c)

    local = [
        pltpu.make_async_copy(fh_hbm, piece(fh, mine), lsem.at[0]),
        pltpu.make_async_copy(x_hbm, piece(xb, mine), lsem.at[1]),
        pltpu.make_async_copy(wupt_hbm, wupt, lsem.at[2]),
        pltpu.make_async_copy(tab_hbm, tab, lsem.at[3]),
        pltpu.make_async_copy(wdn_hbm, wdn, lsem.at[4]),
    ]
    for copy in local:
        copy.start()

    barrier = pltpu.get_barrier_semaphore()
    partners = [sib]
    for k in range(1, 4):
        partners.append(dev((x + k) % 4, y, c, sec))
        partners.append(dev(x, (y + k) % 4, c, sec))
        partners.append(dev(x, y, c, (sec + k) % 4))
    for partner in partners:
        pl.semaphore_signal(barrier, inc=1, device_id=partner, device_id_type=pl.DeviceIdType.MESH)
    pl.semaphore_wait(barrier, len(partners))

    def ag_copy(n, buf, where, chip, cc, s, device):
        xx, yy = chip
        ref = buf.at[where(xx, yy, cc, s)]
        return rc(ref, ref, ag_send.at[n], ag_recv.at[n, s, cidx(xx, yy, cc)], device)

    def ag_first(n, buf, where, s):
        for k in range(1, 4):
            ag_copy(n, buf, where, (x, y), c, s, dev(*at(k, 0), c, sec)).start()
        for k in range(1, 4):
            ag_copy(n, buf, where, (x, y), c, s, dev(*at(0, k), c, sec)).start()
        ag_copy(n, buf, where, (x, y), c, s, sib).start()

    def ag_second(n, buf, where, s):
        for ka in range(1, 4):
            chip = at(4 - ka, 0)
            ag_copy(n, buf, where, chip, c, s, sib).wait_recv()
            for kb in range(1, 4):
                ag_copy(n, buf, where, chip, c, s, dev(*at(0, kb), c, sec)).start()
            ag_copy(n, buf, where, chip, c, s, sib).start()

    def ag_third(n, buf, where, s):
        def body(j, carry):
            chip = at(4 - j // 3, 3 - j % 3)
            ag_copy(n, buf, where, chip, c, s, sib).wait_recv()
            ag_copy(n, buf, where, chip, c, s, sib).start()
            return carry

        lax.fori_loop(0, 12, body, 0)

    def ag_last(n, buf, where, s):
        def body(j, carry):
            ag_copy(n, buf, where, (j // 4, j % 4), 1 - c, s, sib).wait_recv()
            return carry

        lax.fori_loop(0, 16, body, 0)

    def ag_drain(n, buf):
        whole = buf.at[pl.ds(0, 31 * ROWS)]
        rc(whole, whole, ag_send.at[n], ag_recv.at[n, 0, 0], sib).wait_send()

    b_own = y * (1 - c) + x * c

    def rs_copy(n, src, ref, start, count, sem, device, src_start):
        return rc(
            src.at[span(src_start, count)], ref.at[span(start, count)], rs_send.at[n], rs_recv.at[n, sem], device
        )

    def rs_sibling(n, src, s):
        for r in range(2):
            start = ((n * PARTS + s) * 2 + r) * 8 * SUB
            rs_copy(n, src, r0, start, 8 * SUB, s * 11 + r, sib, r * D + s * PART + (1 - c) * 8 * SUB).start()

    def pair_start(ka, u, s):
        aa = (x * (1 - c) + y * c + ka) % 4
        return chain_start(aa * (1 - c) + 2 * u * c, aa * c + 2 * u * (1 - c), c, s)

    def rs_first(n, src, s):
        for r in range(2):
            start = ((n * PARTS + s) * 2 + r) * 8 * SUB
            rs_copy(n, r0, r0, start, 8 * SUB, s * 11 + r, sib, start).wait_recv()
            here = span(r * D + s * PART + c * 8 * SUB, 8 * SUB)
            src[here, :] = (src[here, :].astype(F32) + r0[span(start, 8 * SUB), :].astype(F32)).astype(BF)
        for ka in (2, 1, 3):
            for u in range(2):
                start = ((n * PARTS + s) * 3 + ka - 1) * 4 * SUB + u * 2 * SUB
                rs_copy(
                    n, src, r1, start, 2 * SUB, s * 11 + 2 + (ka - 1) * 2 + u, dev(*at(ka, 0), c, sec),
                    pair_start(ka, u, s),
                ).start()

    def rs_second(n, src, s):
        for u in range(2):
            here = span(pair_start(0, u, s), 2 * SUB)
            total = src[here, :].astype(F32)
            for k in range(3):
                start = ((n * PARTS + s) * 3 + k) * 4 * SUB + u * 2 * SUB
                rs_copy(n, r1, r1, start, 2 * SUB, s * 11 + 2 + k * 2 + u, sib, start).wait_recv()
                total = total + r1[span(start, 2 * SUB), :].astype(F32)
            sums[pl.ds((s * 4 + u * 2) * SUB, 2 * SUB), :] = total
            src[here, :] = total.astype(BF)
        for kb in range(1, 4):
            xx, yy = at(0, kb)
            start = ((n * PARTS + s) * 3 + kb - 1) * SUB
            rs_copy(
                n, src, r2, start, SUB, s * 11 + 7 + kb, dev(xx, yy, c, sec), chain_start(xx, yy, c, s)
            ).start()

    def rs_third(n, s):
        total = sums[span((s * 4 + b_own) * SUB, SUB), :]
        for k in range(3):
            start = ((n * PARTS + s) * 3 + k) * SUB
            rs_copy(n, r2, r2, start, SUB, s * 11 + 8 + k, sib, start).wait_recv()
            total = total + r2[span(start, SUB), :].astype(F32)
        return total

    def rs_drain(n, src):
        whole = src.at[pl.ds(0, 31 * ROWS)]
        rc(whole, whole, rs_send.at[n], rs_recv.at[n, 0], sib).wait_send()

    def ar_peers(phase):
        if phase == 0:
            return [(0, sib)]
        if phase == 1:
            return [(k, dev((x + k) % 4, y, c, sec)) for k in (1, 2, 3)]
        if phase == 2:
            return [(3 + k, dev(x, (y + k) % 4, c, sec)) for k in (1, 2, 3)]
        return [(6 + k, dev(x, y, c, (sec + k) % 4)) for k in (1, 2, 3)]

    def ar_copies(n, cur, slot, phase):
        return [
            rc(cur.at[phase], slot.at[s], ar_send.at[n], ar_recv.at[n, s], device)
            for s, device in ar_peers(phase)
        ]

    def ar_start(n, cur, slot, phase):
        for copy in ar_copies(n, cur, slot, phase):
            copy.start()

    def ar_wait(n, cur, slot, phase):
        for copy in ar_copies(n, cur, slot, phase):
            copy.wait_recv()

    def ar_sum(n, cur, slot, phase):
        ar_wait(n, cur, slot, phase)
        total = cur[phase].astype(F32)
        for s, _ in ar_peers(phase):
            total = total + slot[s].astype(F32)
        cur[phase + 1] = total.astype(cur.dtype)

    def ar_drain(n, slot, count):
        part = slot.at[pl.ds(0, count)]
        rc(part, part, ar_send.at[n], ar_recv.at[n, 0], sib).wait_send()

    def feature_half(buf, h):
        return jnp.concatenate([buf[pl.ds(h * HALF, HALF), :], buf[pl.ds(D + h * HALF, HALF), :]], axis=1)

    local[0].wait()
    for s in range(PARTS):
        ag_first(0, fh, given, s)
    local[1].wait()

    columns = ((sec * 16 + ten) * 2 + dp) * VROWS + lax.broadcasted_iota(jnp.int32, (VROWS, TOK), 0)
    dim_part = dot(pdim[...], fh[rows(mine), :])
    dim_part = jnp.where(sec == 0, dim_part, jnp.zeros_like(dim_part))
    blank = jnp.zeros_like(dim_part)
    sm_cur[0, 0:RANK, 0:SEQ] = jnp.where(dp == 0, dim_part, blank).astype(BF)
    sm_cur[0, 0:RANK, SEQ:TOK] = jnp.where(dp == 1, dim_part, blank).astype(BF)
    token_hot = jnp.where(tok[...] == columns, 1.0, 0.0).astype(BF)
    sm_cur[0, RANK:2 * RANK, :] = dot(pvoc[...], token_hot).astype(BF)

    pdt[rows(mine), :] = jnp.concatenate([pdim[...].T, jnp.zeros((ROWS, SEQ - RANK), BF)], axis=1)

    for s in range(PARTS):
        ag_second(0, fh, given, s)
    ar_start(0, sm_cur, sm_slot, 0)
    local[2].wait()

    def turn(b, carry):
        k0 = pl.multiple_of(b * TB, TB)
        wup[pl.ds(k0, TB), :] = wupt[:, pl.ds(k0, TB)].T
        return carry

    lax.fori_loop(0, D // TB, turn, 0)
    for s in range(PARTS):
        ag_third(0, fh, given, s)
    for s in range(PARTS):
        ag_first(1, xb, given, s)
    for s in range(PARTS):
        ag_last(0, fh, given, s)

    local[3].wait()
    logits[...] = dot(tab[:, 0:HALF], feature_half(fh, 0))
    logits[...] += dot(tab[:, HALF:D], feature_half(fh, 1))

    peak = jnp.max(logits[...], axis=0, keepdims=True)
    st_cur[0] = jnp.zeros((8, TOK), F32)
    st_cur[0, 0:1, :] = peak
    st_cur[0, 1:2, :] = jnp.sum(jnp.exp(logits[...] - peak), axis=0, keepdims=True)
    ar_start(1, st_cur, st_slot, 0)

    def stats_step(phase):
        ar_wait(1, st_cur, st_slot, phase)
        peaks = [st_cur[phase, 0:1, :]] + [st_slot[s, 0:1, :] for s, _ in ar_peers(phase)]
        sums = [st_cur[phase, 1:2, :]] + [st_slot[s, 1:2, :] for s, _ in ar_peers(phase)]
        top = peaks[0]
        for other in peaks[1:]:
            top = jnp.maximum(top, other)
        total = jnp.zeros_like(top)
        for a, b in zip(peaks, sums):
            total = total + b * jnp.exp(a - top)
        st_cur[phase + 1] = jnp.zeros((8, TOK), F32)
        st_cur[phase + 1, 0:1, :] = top
        st_cur[phase + 1, 1:2, :] = total
        if phase < 3:
            ar_start(1, st_cur, st_slot, phase + 1)

    stats_step(0)
    for s in range(PARTS):
        ag_second(1, xb, given, s)
    ar_sum(0, sm_cur, sm_slot, 0)
    ar_start(0, sm_cur, sm_slot, 1)
    stats_step(1)
    stats_step(2)
    ag_drain(0, fh)
    stats_step(3)

    top = st_cur[4, 0:1, :]
    scale = 1.0 / st_cur[4, 1:2, :]
    hot = jnp.where(tgt[...] == columns, 1.0, 0.0)
    grad = jnp.exp(logits[...] - top) * scale - hot
    logits[...] = grad
    gradt[...] = grad.T.astype(BF)

    def head_step(b, carry):
        k0 = pl.multiple_of(b * HB, HB)
        k1 = pl.multiple_of(D + b * HB, 16)
        block = dot(gradt[...], tab[:, pl.ds(k0, HB)]).T.astype(BF)
        fh[pl.ds(k0, HB), :] = block[:, 0:SEQ]
        fh[pl.ds(k1, HB), :] = block[:, SEQ:TOK]
        return carry

    steps = PART // HB
    for s in range(PARTS):
        lax.fori_loop(s * steps, (s + 1) * steps, head_step, 0)
        rs_sibling(0, fh, s)
        if s:
            rs_first(0, fh, s - 1)
    rs_first(0, fh, PARTS - 1)

    ar_sum(0, sm_cur, sm_slot, 1)
    ar_start(0, sm_cur, sm_slot, 2)
    for s in range(PARTS):
        ag_third(1, xb, given, s)
    for s in range(PARTS):
        ag_last(1, xb, given, s)
    hidden = dot(wupt[:, 0:HALF], feature_half(xb, 0)) + dot(wupt[:, HALF:D], feature_half(xb, 1))
    gate = jax.nn.sigmoid(hidden)
    slope[...] = gate * (1.0 + hidden * (1.0 - gate))
    inproj[...] = dot(pin[...], (hidden * gate).astype(BF))
    ar_sum(0, sm_cur, sm_slot, 2)
    ar_start(0, sm_cur, sm_slot, 3)

    def own_rows(k, s):
        return pl.ds(k * ROWS + s * SUB, SUB)

    def head_done(s):
        total = rs_third(0, s)

        @pl.when(sec == 3)
        def _():
            own[own_rows(0, s), :] = total

        @pl.when(sec != 3)
        def _():
            zr[own_rows(3, s), :] = total.astype(BF)
            rc(
                zr.at[own_rows(3, s)], zr.at[span(sec * ROWS + s * SUB, SUB)], z_send, z_recv.at[s, sec],
                dev(x, y, c, 3),
            ).start()

    def begin_last(s):
        total = own[own_rows(0, s), :]
        for z in range(3):
            held = zr.at[own_rows(z, s)]
            rc(held, held, z_send, z_recv.at[s, z], sib).wait_recv()
            total = total + zr[own_rows(z, s), :].astype(F32)
        cot[chained(x, y, c, s), :] = total.astype(BF)
        ag_first(2, cot, chained, s)

    def begin(s):
        held = cot.at[chained(x, y, c, s)]
        rc(held, held, c_send, c_recv.at[s], sib).wait_recv()
        ag_first(2, cot, chained, s)

    rs_second(0, fh, 0)
    rs_second(0, fh, 1)
    head_done(0)
    rs_second(0, fh, 2)
    head_done(1)
    local[4].wait()
    ag_drain(1, xb)

    @pl.when(sec == 3)
    def _():
        begin_last(0)

    head_done(2)

    @pl.when(sec == 3)
    def _():
        begin_last(1)
        ag_second(2, cot, chained, 0)
        begin_last(2)

    @pl.when(sec != 3)
    def _():
        @pl.when(sec == 0)
        def _():
            for s in range(PARTS):
                ag_first(3, pdt, given, s)
            for s in range(PARTS):
                ag_second(3, pdt, given, s)
            for s in range(PARTS):
                ag_third(3, pdt, given, s)
            for s in range(PARTS):
                ag_last(3, pdt, given, s)
            upside[...] = dot(wupt[...], pdt[0:D, :]).T[0:RANK, :].astype(BF)

        begin(0)
        begin(1)
        ag_second(2, cot, chained, 0)
        begin(2)

    def down(s):
        right = jnp.concatenate(
            [cot[pl.ds(s * PART, PART), :], cot[pl.ds(D + s * PART, PART), :]], axis=1
        )
        return dot(wdn[:, s * PART:(s + 1) * PART], right)

    ag_second(2, cot, chained, 1)
    ag_third(2, cot, chained, 0)
    ag_second(2, cot, chained, 2)
    ag_last(2, cot, chained, 0)
    act[...] = down(0)
    ag_third(2, cot, chained, 1)
    ag_last(2, cot, chained, 1)
    act[...] += down(1)
    ag_third(2, cot, chained, 2)
    ag_last(2, cot, chained, 2)
    total_act = act[...] + down(2)
    hgrad[...] = (total_act * slope[...]).astype(BF)

    def back(s):
        block = dot(wup[s * PART:(s + 1) * PART, :], hgrad[...]).astype(BF)
        xb[pl.ds(s * PART, PART), :] = block[:, 0:SEQ]
        xb[pl.ds(D + s * PART, PART), :] = block[:, SEQ:TOK]

    def section_grads():
        outproj = dot(pout[:, 0:HALF], feature_half(cot, 0)) + dot(pout[:, HALF:D], feature_half(cot, 1))
        la_cur[0] = outer_pair(outproj, inproj[...])
        ar_start(2, la_cur, la_slot, 0)

    def table_part():
        vside[...] = dot(pvoc[...], logits[...].astype(BF))
        ar_sum(0, sm_cur, sm_slot, 3)
        ta_cur[0] = outer_pair(vside[...], sm_cur[4, 0:RANK, :].astype(F32))

    def relay_done(s):
        total = rs_third(1, s) + cot[chained(x, y, c, s), :].astype(F32)
        zr[own_rows(4, s), :] = total.astype(BF)
        rc(
            zr.at[own_rows(4, s)], cot.at[chained(x, y, c, s)], c_send, c_recv.at[s], dev(x, y, c, (sec + 3) % 4)
        ).start()

    @pl.when(sec != 0)
    def _():
        for s in range(PARTS):
            back(s)
            rs_sibling(1, xb, s)
            if s:
                rs_first(1, xb, s - 1)
        rs_first(1, xb, PARTS - 1)
        section_grads()
        rs_second(1, xb, 0)
        rs_second(1, xb, 1)
        relay_done(0)
        rs_second(1, xb, 2)
        relay_done(1)
        relay_done(2)
        table_part()

    @pl.when(sec == 0)
    def _():
        table_part()
        embed = dot(upside[...], hgrad[...])
        for r in range(2):
            side = embed[:, r * SEQ:(r + 1) * SEQ]
            for s in range(PARTS):
                here = span(chain_start(x, y, c, s) - dp * D, SUB)
                term = dot(pdt[here, :], cot[chained(x, y, c, s), :], ((0,), (0,)))[0:RANK, :]
                side = side + jnp.where(dp == r, term, jnp.zeros_like(term))
            token = sm_cur[4, RANK:2 * RANK, r * SEQ:(r + 1) * SEQ].astype(F32)
            ta_cur[0, :, r * RANK:(r + 1) * RANK] += math.sqrt(D) * dot(
                token, side, ((1,), (1,)), lax.Precision.HIGHEST
            )

    ar_start(3, ta_cur, ta_slot, 0)

    @pl.when(sec == 0)
    def _():
        section_grads()

    for phase in range(3):
        ar_sum(3, ta_cur, ta_slot, phase)
        ar_start(3, ta_cur, ta_slot, phase + 1)
        ar_sum(2, la_cur, la_slot, phase)
        if phase < 2:
            ar_start(2, la_cur, la_slot, phase + 1)
    lay_out[...] = jnp.where(dp == 0, la_cur[3, :, 0:RANK], la_cur[3, :, RANK:2 * RANK])

    ag_drain(2, cot)
    rs_drain(0, fh)
    ar_drain(0, sm_slot, 10)
    ar_drain(1, st_slot, 10)
    ar_drain(2, la_slot, 7)

    @pl.when(sec != 3)
    def _():
        rc(piece(zr, 3), piece(zr, 3), z_send, z_recv.at[0, 0], sib).wait_send()

    @pl.when(sec != 0)
    def _():
        rc(piece(zr, 4), piece(zr, 4), c_send, c_recv.at[0], sib).wait_send()
        rs_drain(1, xb)

    @pl.when(sec == 0)
    def _():
        ag_drain(3, pdt)

    ar_sum(3, ta_cur, ta_slot, 3)
    tab_out[...] = jnp.where(dp == 0, ta_cur[4, :, 0:RANK], ta_cur[4, :, RANK:2 * RANK])
    ar_drain(3, ta_slot, 10)


def shards(x_in, final_hidden, w_up, w_down, table, token_ids, targets, proj_in, proj_out, proj_vocab, proj_dim):
    vmem = pl.BlockSpec(memory_space=pltpu.VMEM)
    hbm = pl.BlockSpec(memory_space=pl.ANY)
    full = lambda n: pltpu.VMEM((n * ROWS, SEQ), BF)
    dma = pltpu.SemaphoreType.DMA
    layer, tab = pl.pallas_call(
        kernel,
        out_shape=[jax.ShapeDtypeStruct((RANK, RANK), F32)] * 2,
        in_specs=[hbm] * 5 + [vmem] * 6,
        out_specs=[vmem] * 2,
        scratch_shapes=[
            pltpu.VMEM((VROWS, D), BF),
            pltpu.VMEM((UNITS, D), BF),
            pltpu.VMEM((D, UNITS), BF),
            pltpu.VMEM((UNITS, D), BF),
            full(32), full(32), full(32), full(32),
            full(2 * 16), full(2 * 12), full(2 * 3), full(5),
            pltpu.VMEM((VROWS, TOK), F32),
            pltpu.VMEM((TOK, VROWS), BF),
            pltpu.VMEM((UNITS, TOK), F32),
            pltpu.VMEM((UNITS, TOK), F32),
            pltpu.VMEM((UNITS, TOK), BF),
            pltpu.VMEM((RANK, TOK), F32),
            pltpu.VMEM((RANK, TOK), F32),
            pltpu.VMEM((RANK, UNITS), BF),
            pltpu.VMEM((ROWS, SEQ), F32),
            pltpu.VMEM((4 * ROWS, SEQ), F32),
            pltpu.VMEM((5, 2 * RANK, TOK), BF),
            pltpu.VMEM((10, 2 * RANK, TOK), BF),
            pltpu.VMEM((5, 8, TOK), F32),
            pltpu.VMEM((10, 8, TOK), F32),
            pltpu.VMEM((5, RANK, 2 * RANK), F32),
            pltpu.VMEM((10, RANK, 2 * RANK), F32),
            pltpu.VMEM((5, RANK, 2 * RANK), F32),
            pltpu.VMEM((10, RANK, 2 * RANK), F32),
            dma((5,)),
            dma((4,)), dma((4, PARTS, 32)),
            dma((2,)), dma((2, 11 * PARTS)),
            dma(()), dma((PARTS, 3)),
            dma(()), dma((PARTS,)),
            dma((4,)), dma((4, 10)),
        ],
        compiler_params=pltpu.CompilerParams(
            collective_id=0, has_side_effects=True, vmem_limit_bytes=62 * 1024 * 1024
        ),
    )(
        x_in[0], final_hidden, jnp.swapaxes(w_up[0], 0, 1), w_down[0], table,
        token_ids.reshape(1, TOK), targets.reshape(1, TOK),
        proj_in[0], proj_out[0], proj_vocab, proj_dim,
    )
    return layer[None, None], tab[None]


def solution(mesh):
    placed = (
        P("section", "tensor", "dp"),
        P("tensor", "dp"),
        P("section", None, ("tensor", "dp")),
        P("section", ("tensor", "dp"), None),
        P(("section", "tensor", "dp"), None),
        P(),
        P(),
        P("section", None, ("tensor", "dp")),
        P("section", None, None),
        P(None, ("section", "tensor", "dp")),
        P(None, "tensor"),
    )
    return jax.shard_map(
        shards,
        mesh=mesh,
        in_specs=placed,
        out_specs=(P("section", "dp", None, None), P("dp", None, None)),
        check_vma=False,
    )
```

```python
import math

import jax
import jax.numpy as jnp
from jax import lax
from jax.experimental import pallas as pl
from jax.experimental.pallas import tpu as pltpu
from jax.sharding import PartitionSpec as P

D = 5376
TOK = 256
SEQ = 128
RANK = 64
UNITS = 672
VROWS = 1024
ROWS = 336
PARTS = 3
SUB = ROWS // PARTS
PART = D // PARTS
HALF = D // 2
FOLD = RANK // 2
TB = 384
HB = 896
BF = jnp.bfloat16
F32 = jnp.float32


def dot(a, b, dims=((1,), (0,)), precision=None):
    return lax.dot_general(a, b, (dims, ((), ())), preferred_element_type=F32, precision=precision)


def outer_pair(left, right):
    parts = [
        fold(dot(left[:, q * SEQ:(q + 1) * SEQ], right[:, q * SEQ:(q + 1) * SEQ], ((1,), (1,)), lax.Precision.HIGHEST))
        for q in range(2)
    ]
    return jnp.concatenate(parts, axis=0)


def fold(square):
    return jnp.concatenate([square[0:FOLD, :], square[FOLD:RANK, :]], axis=1)


def kernel(
    x_hbm, fh_hbm, wupt_hbm, wdn_hbm, tab_hbm, tok, tgt, pin, pout, pvoc, pdim,
    lay_out, tab_out,
    tab, wupt, wup, wdn, fh, xb, cot, pdt,
    r0, r1, r2, zr,
    logits, gradt, act, slope, hgrad, inproj, vside, upside, own, sums,
    sm_cur, sm_slot, st_cur, st_slot, la_cur, la_slot, ta_cur, ta_slot,
    lsem, ag_send, ag_recv, rs_send, rs_recv, z_send, z_recv, c_send, c_recv, ar_send, ar_recv,
):
    sec = lax.axis_index("section")
    ten = lax.axis_index("tensor")
    dp = lax.axis_index("dp")
    c = ten % 2
    y = (ten // 2) % 4
    lo = ten // 8
    x = dp * 2 + lo

    def dev(xx, yy, cc, zz):
        return (zz, (xx % 2) * 8 + yy * 2 + cc, xx // 2)

    def at(ka, kb):
        return (x + ka * (1 - c) + kb * c) % 4, (y + ka * c + kb * (1 - c)) % 4

    def cidx(xx, yy, cc):
        return xx * 8 + yy * 2 + cc

    def rows(i):
        return pl.ds(pl.multiple_of(i * ROWS, 16), ROWS)

    def piece(ref, i):
        return ref.at[rows(i)]

    def span(start, count):
        return pl.ds(pl.multiple_of(start, 16), count)

    def given(xx, yy, cc, s):
        return span((xx * 8 + yy * 2 + cc) * ROWS + s * SUB, SUB)

    def chain_start(xx, yy, cc, s):
        spot = (1 - cc) * ((xx % 2) * 4 + yy) + cc * (yy * 2 + xx % 2)
        return (xx // 2) * D + s * PART + (cc * 8 + spot) * SUB

    def chained(xx, yy, cc, s):
        return span(chain_start(xx, yy, cc, s), SUB)

    def rc(src, dst, ssem, rsem, device):
        return pltpu.make_async_remote_copy(
            src_ref=src, dst_ref=dst, send_sem=ssem, recv_sem=rsem,
            device_id=device, device_id_type=pl.DeviceIdType.MESH,
        )

    sib = dev(x, y, 1 - c, sec)
    mine = cidx(x, y, c)

    local = [
        pltpu.make_async_copy(fh_hbm, piece(fh, mine), lsem.at[0]),
        pltpu.make_async_copy(x_hbm, piece(xb, mine), lsem.at[1]),
        pltpu.make_async_copy(wupt_hbm, wupt, lsem.at[2]),
        pltpu.make_async_copy(tab_hbm, tab, lsem.at[3]),
        pltpu.make_async_copy(wdn_hbm, wdn, lsem.at[4]),
    ]
    for copy in local:
        copy.start()

    barrier = pltpu.get_barrier_semaphore()
    partners = [sib]
    for k in range(1, 4):
        partners.append(dev((x + k) % 4, y, c, sec))
        partners.append(dev(x, (y + k) % 4, c, sec))
        partners.append(dev(x, y, c, (sec + k) % 4))
        for j in range(1, 4):
            partners.append(dev((x + j) % 4, (y + k) % 4, c, sec))
    for partner in partners:
        pl.semaphore_signal(barrier, inc=1, device_id=partner, device_id_type=pl.DeviceIdType.MESH)
    pl.semaphore_wait(barrier, len(partners))

    def ag_copy(n, buf, where, chip, cc, s, device):
        xx, yy = chip
        ref = buf.at[where(xx, yy, cc, s)]
        return rc(ref, ref, ag_send.at[n], ag_recv.at[n, s, cidx(xx, yy, cc)], device)

    def ag_first(n, buf, where, s):
        for k in range(1, 4):
            ag_copy(n, buf, where, (x, y), c, s, dev(*at(k, 0), c, sec)).start()
        for k in range(1, 4):
            ag_copy(n, buf, where, (x, y), c, s, dev(*at(0, k), c, sec)).start()
        ag_copy(n, buf, where, (x, y), c, s, sib).start()

    def ag_second(n, buf, where, s):
        for ka in range(1, 4):
            chip = at(4 - ka, 0)
            ag_copy(n, buf, where, chip, c, s, sib).wait_recv()
            for kb in range(1, 4):
                ag_copy(n, buf, where, chip, c, s, dev(*at(0, kb), c, sec)).start()
            ag_copy(n, buf, where, chip, c, s, sib).start()

    def ag_third(n, buf, where, s):
        def body(j, carry):
            chip = at(4 - j // 3, 3 - j % 3)
            ag_copy(n, buf, where, chip, c, s, sib).wait_recv()
            ag_copy(n, buf, where, chip, c, s, sib).start()
            return carry

        lax.fori_loop(0, 12, body, 0)

    def ag_last(n, buf, where, s):
        def body(j, carry):
            ag_copy(n, buf, where, (j // 4, j % 4), 1 - c, s, sib).wait_recv()
            return carry

        lax.fori_loop(0, 16, body, 0)

    def ag_drain(n, buf):
        whole = buf.at[pl.ds(0, 31 * ROWS)]
        rc(whole, whole, ag_send.at[n], ag_recv.at[n, 0, 0], sib).wait_send()

    b_own = y * (1 - c) + x * c

    def rs_copy(n, src, ref, start, count, sem, device, src_start):
        return rc(
            src.at[span(src_start, count)], ref.at[span(start, count)], rs_send.at[n], rs_recv.at[n, sem], device
        )

    def rs_sibling(n, src, s):
        for r in range(2):
            start = ((n * PARTS + s) * 2 + r) * 8 * SUB
            rs_copy(n, src, r0, start, 8 * SUB, s * 11 + r, sib, r * D + s * PART + (1 - c) * 8 * SUB).start()

    def run_start(ka, u, s):
        aa = (x * (1 - c) + y * c + ka) % 4
        return chain_start(aa * (1 - c) + 2 * u * c, aa * c + 2 * u * (1 - c), c, s)

    def rs_first(n, src, s):
        for r in range(2):
            start = ((n * PARTS + s) * 2 + r) * 8 * SUB
            rs_copy(n, r0, r0, start, 8 * SUB, s * 11 + r, sib, start).wait_recv()
            here = span(r * D + s * PART + c * 8 * SUB, 8 * SUB)
            src[here, :] = (src[here, :].astype(F32) + r0[span(start, 8 * SUB), :].astype(F32)).astype(BF)
        for ka in (2, 1, 3):
            for u in range(2):
                start = ((n * PARTS + s) * 3 + ka - 1) * 4 * SUB + u * 2 * SUB
                rs_copy(
                    n, src, r1, start, 2 * SUB, s * 11 + 2 + (ka - 1) * 2 + u, dev(*at(ka, 0), c, sec),
                    run_start(ka, u, s),
                ).start()

    def rs_second(n, src, s):
        for u in range(2):
            here = span(run_start(0, u, s), 2 * SUB)
            total = src[here, :].astype(F32)
            for k in range(3):
                start = ((n * PARTS + s) * 3 + k) * 4 * SUB + u * 2 * SUB
                rs_copy(n, r1, r1, start, 2 * SUB, s * 11 + 2 + k * 2 + u, sib, start).wait_recv()
                total = total + r1[span(start, 2 * SUB), :].astype(F32)
            sums[pl.ds((s * 4 + u * 2) * SUB, 2 * SUB), :] = total
            src[here, :] = total.astype(BF)
        for kb in range(1, 4):
            xx, yy = at(0, kb)
            start = ((n * PARTS + s) * 3 + kb - 1) * SUB
            rs_copy(
                n, src, r2, start, SUB, s * 11 + 7 + kb, dev(xx, yy, c, sec), chain_start(xx, yy, c, s)
            ).start()

    def rs_third(n, s):
        total = sums[span((s * 4 + b_own) * SUB, SUB), :]
        for k in range(3):
            start = ((n * PARTS + s) * 3 + k) * SUB
            rs_copy(n, r2, r2, start, SUB, s * 11 + 8 + k, sib, start).wait_recv()
            total = total + r2[span(start, SUB), :].astype(F32)
        return total

    def rs_drain(n, src):
        whole = src.at[pl.ds(0, 31 * ROWS)]
        rc(whole, whole, rs_send.at[n], rs_recv.at[n, 0], sib).wait_send()

    def ar_peers(phase):
        if phase == 0:
            return [(0, sib)]
        if phase == 1:
            return [(k, dev((x + k) % 4, y, c, sec)) for k in (1, 2, 3)]
        if phase == 2:
            return [(3 + k, dev(x, (y + k) % 4, c, sec)) for k in (1, 2, 3)]
        return [(6 + k, dev(x, y, c, (sec + k) % 4)) for k in (1, 2, 3)]

    def ar_copies(n, cur, slot, phase):
        return [
            rc(cur.at[phase], slot.at[s], ar_send.at[n], ar_recv.at[n, s], device)
            for s, device in ar_peers(phase)
        ]

    def ar_start(n, cur, slot, phase):
        for copy in ar_copies(n, cur, slot, phase):
            copy.start()

    def ar_wait(n, cur, slot, phase):
        for copy in ar_copies(n, cur, slot, phase):
            copy.wait_recv()

    def ar_sum(n, cur, slot, phase):
        ar_wait(n, cur, slot, phase)
        total = cur[phase].astype(F32)
        for s, _ in ar_peers(phase):
            total = total + slot[s].astype(F32)
        cur[phase + 1] = total.astype(cur.dtype)

    def pair_copies(n, cur, slot, phase):
        copies = []
        for s, device in ar_peers(phase):
            if phase == 0:
                src, dst = cur.at[0], slot.at[0]
            elif phase == 1:
                src = cur.at[1, pl.ds(pl.multiple_of(((x + s) % 4) // 2 * FOLD, FOLD), FOLD)]
                dst = slot.at[s, pl.ds(0, FOLD)]
            else:
                src, dst = cur.at[phase, pl.ds(0, FOLD)], slot.at[s, pl.ds(0, FOLD)]
            copies.append(rc(src, dst, ar_send.at[n], ar_recv.at[n, s], device))
        return copies

    def pair_start(n, cur, slot, phase):
        for copy in pair_copies(n, cur, slot, phase):
            copy.start()

    def pair_sum(n, cur, slot, phase):
        for copy in pair_copies(n, cur, slot, phase):
            copy.wait_recv()
        if phase == 0:
            cur[1] = cur[0] + slot[0]
            return
        total = cur[1, pl.ds(pl.multiple_of(dp * FOLD, FOLD), FOLD), :] if phase == 1 else cur[phase, 0:FOLD, :]
        for s, _ in ar_peers(phase):
            total = total + slot[s, 0:FOLD, :]
        cur[phase + 1, 0:FOLD, :] = total

    def pair_drain(n, slot, count):
        part = slot.at[pl.ds(0, 1)]
        rc(part, part, ar_send.at[n], ar_recv.at[n, 0], sib).wait_send()
        part = slot.at[pl.ds(1, count), pl.ds(0, FOLD)]
        rc(part, part, ar_send.at[n], ar_recv.at[n, 0], sib).wait_send()

    def unfold(out, cur, phase):
        out[0:FOLD, :] = cur[phase, 0:FOLD, 0:RANK]
        out[FOLD:RANK, :] = cur[phase, 0:FOLD, RANK:2 * RANK]

    def ar_drain(n, slot, count):
        part = slot.at[pl.ds(0, count)]
        rc(part, part, ar_send.at[n], ar_recv.at[n, 0], sib).wait_send()

    def feature_half(buf, h):
        return jnp.concatenate([buf[pl.ds(h * HALF, HALF), :], buf[pl.ds(D + h * HALF, HALF), :]], axis=1)

    local[0].wait()
    for s in range(PARTS):
        ag_first(0, fh, given, s)
    local[1].wait()

    columns = ((sec * 16 + ten) * 2 + dp) * VROWS + lax.broadcasted_iota(jnp.int32, (VROWS, TOK), 0)
    dim_part = dot(pdim[...], fh[rows(mine), :])
    dim_part = jnp.where(sec == 0, dim_part, jnp.zeros_like(dim_part))
    blank = jnp.zeros_like(dim_part)
    sm_cur[0, 0:RANK, 0:SEQ] = jnp.where(dp == 0, dim_part, blank).astype(BF)
    sm_cur[0, 0:RANK, SEQ:TOK] = jnp.where(dp == 1, dim_part, blank).astype(BF)
    token_hot = jnp.where(tok[...] == columns, 1.0, 0.0).astype(BF)
    sm_cur[0, RANK:2 * RANK, :] = dot(pvoc[...], token_hot).astype(BF)

    pdt[rows(mine), :] = jnp.concatenate([pdim[...].T, jnp.zeros((ROWS, SEQ - RANK), BF)], axis=1)

    for s in range(PARTS):
        ag_second(0, fh, given, s)
    ar_start(0, sm_cur, sm_slot, 0)
    local[2].wait()

    def turn(b, carry):
        k0 = pl.multiple_of(b * TB, TB)
        wup[pl.ds(k0, TB), :] = wupt[:, pl.ds(k0, TB)].T
        return carry

    lax.fori_loop(0, D // TB, turn, 0)
    for s in range(PARTS):
        ag_third(0, fh, given, s)
    for s in range(PARTS):
        ag_first(1, xb, given, s)
    for s in range(PARTS):
        ag_last(0, fh, given, s)

    local[3].wait()
    logits[...] = dot(tab[:, 0:HALF], feature_half(fh, 0))
    logits[...] += dot(tab[:, HALF:D], feature_half(fh, 1))

    peak = jnp.max(logits[...], axis=0, keepdims=True)
    st_cur[0] = jnp.zeros((8, TOK), F32)
    st_cur[0, 0:1, :] = peak
    st_cur[0, 1:2, :] = jnp.sum(jnp.exp(logits[...] - peak), axis=0, keepdims=True)

    def stats_peers(phase):
        if phase == 0:
            return [(0, sib)]
        if phase == 1:
            return [
                (4 * i + j, dev((x + i) % 4, (y + j) % 4, c, sec)) for i in (2, 1, 3, 0) for j in (2, 1, 3, 0) if i or j
            ]
        return [(15 + k, dev(x, y, c, (sec + k) % 4)) for k in (2, 1, 3)]

    def stats_copies(phase):
        return [
            rc(st_cur.at[phase], st_slot.at[s], ar_send.at[1], ar_recv.at[1, s], device)
            for s, device in stats_peers(phase)
        ]

    def stats_step(phase):
        for copy in stats_copies(phase):
            copy.wait_recv()
        peaks = [st_cur[phase, 0:1, :]] + [st_slot[s, 0:1, :] for s, _ in stats_peers(phase)]
        sums = [st_cur[phase, 1:2, :]] + [st_slot[s, 1:2, :] for s, _ in stats_peers(phase)]
        top = peaks[0]
        for other in peaks[1:]:
            top = jnp.maximum(top, other)
        total = jnp.zeros_like(top)
        for a, b in zip(peaks, sums):
            total = total + b * jnp.exp(a - top)
        st_cur[phase + 1] = jnp.zeros((8, TOK), F32)
        st_cur[phase + 1, 0:1, :] = top
        st_cur[phase + 1, 1:2, :] = total
        if phase < 2:
            for copy in stats_copies(phase + 1):
                copy.start()

    for copy in stats_copies(0):
        copy.start()
    stats_step(0)
    for s in range(PARTS):
        ag_second(1, xb, given, s)
    ar_sum(0, sm_cur, sm_slot, 0)
    ar_start(0, sm_cur, sm_slot, 1)
    stats_step(1)
    ag_drain(0, fh)
    stats_step(2)

    top = st_cur[3, 0:1, :]
    scale = 1.0 / st_cur[3, 1:2, :]
    hot = jnp.where(tgt[...] == columns, 1.0, 0.0)
    grad = jnp.exp(logits[...] - top) * scale - hot
    logits[...] = grad
    gradt[...] = grad.T.astype(BF)

    def head_step(b, carry):
        k0 = pl.multiple_of(b * HB, HB)
        k1 = pl.multiple_of(D + b * HB, 16)
        block = dot(gradt[...], tab[:, pl.ds(k0, HB)]).T.astype(BF)
        fh[pl.ds(k0, HB), :] = block[:, 0:SEQ]
        fh[pl.ds(k1, HB), :] = block[:, SEQ:TOK]
        return carry

    steps = PART // HB
    for s in range(PARTS):
        lax.fori_loop(s * steps, (s + 1) * steps, head_step, 0)
        rs_sibling(0, fh, s)
        if s:
            rs_first(0, fh, s - 1)
    rs_first(0, fh, PARTS - 1)

    ar_sum(0, sm_cur, sm_slot, 1)
    ar_start(0, sm_cur, sm_slot, 2)
    for s in range(PARTS):
        ag_third(1, xb, given, s)
    for s in range(PARTS):
        ag_last(1, xb, given, s)
    hidden = dot(wupt[:, 0:HALF], feature_half(xb, 0)) + dot(wupt[:, HALF:D], feature_half(xb, 1))
    gate = jax.nn.sigmoid(hidden)
    slope[...] = gate * (1.0 + hidden * (1.0 - gate))
    inproj[...] = dot(pin[...], (hidden * gate).astype(BF))
    ar_sum(0, sm_cur, sm_slot, 2)
    ar_start(0, sm_cur, sm_slot, 3)

    def own_rows(k, s):
        return pl.ds(k * ROWS + s * SUB, SUB)

    def head_done(s):
        total = rs_third(0, s)

        @pl.when(sec == 3)
        def _():
            own[own_rows(0, s), :] = total

        @pl.when(sec != 3)
        def _():
            zr[own_rows(3, s), :] = total.astype(BF)
            rc(
                zr.at[own_rows(3, s)], zr.at[span(sec * ROWS + s * SUB, SUB)], z_send, z_recv.at[s, sec],
                dev(x, y, c, 3),
            ).start()

    def begin_last(s):
        total = own[own_rows(0, s), :]
        for z in range(3):
            held = zr.at[own_rows(z, s)]
            rc(held, held, z_send, z_recv.at[s, z], sib).wait_recv()
            total = total + zr[own_rows(z, s), :].astype(F32)
        cot[chained(x, y, c, s), :] = total.astype(BF)
        ag_first(2, cot, chained, s)

    def begin(s):
        held = cot.at[chained(x, y, c, s)]
        rc(held, held, c_send, c_recv.at[s], sib).wait_recv()
        ag_first(2, cot, chained, s)

    rs_second(0, fh, 0)
    rs_second(0, fh, 1)
    head_done(0)
    rs_second(0, fh, 2)
    head_done(1)
    local[4].wait()
    ag_drain(1, xb)

    @pl.when(sec == 3)
    def _():
        begin_last(0)

    head_done(2)

    @pl.when(sec == 3)
    def _():
        begin_last(1)
        ag_second(2, cot, chained, 0)
        begin_last(2)

    @pl.when(sec != 3)
    def _():
        @pl.when(sec == 0)
        def _():
            for s in range(PARTS):
                ag_first(3, pdt, given, s)
            for s in range(PARTS):
                ag_second(3, pdt, given, s)
            for s in range(PARTS):
                ag_third(3, pdt, given, s)
            for s in range(PARTS):
                ag_last(3, pdt, given, s)
            upside[...] = dot(wupt[...], pdt[0:D, :]).T[0:RANK, :].astype(BF)

        begin(0)
        begin(1)
        ag_second(2, cot, chained, 0)
        begin(2)

    def down(s, cc):
        k0 = pl.multiple_of(s * PART + cc * (PART // 2), 128)
        k1 = pl.multiple_of(D + s * PART + cc * (PART // 2), 16)
        right = jnp.concatenate([cot[pl.ds(k0, PART // 2), :], cot[pl.ds(k1, PART // 2), :]], axis=1)
        return dot(wdn[:, pl.ds(k0, PART // 2)], right)

    ag_second(2, cot, chained, 1)
    ag_third(2, cot, chained, 0)
    ag_second(2, cot, chained, 2)
    act[...] = down(0, c)
    ag_last(2, cot, chained, 0)
    act[...] += down(0, 1 - c)
    ag_third(2, cot, chained, 1)
    act[...] += down(1, c)
    ag_last(2, cot, chained, 1)
    act[...] += down(1, 1 - c)
    ag_third(2, cot, chained, 2)
    act[...] += down(2, c)
    ag_last(2, cot, chained, 2)
    total_act = act[...] + down(2, 1 - c)
    hgrad[...] = (total_act * slope[...]).astype(BF)

    def back(s):
        block = dot(wup[s * PART:(s + 1) * PART, :], hgrad[...]).astype(BF)
        xb[pl.ds(s * PART, PART), :] = block[:, 0:SEQ]
        xb[pl.ds(D + s * PART, PART), :] = block[:, SEQ:TOK]

    def section_grads():
        outproj = dot(pout[:, 0:HALF], feature_half(cot, 0)) + dot(pout[:, HALF:D], feature_half(cot, 1))
        la_cur[0] = outer_pair(outproj, inproj[...])
        pair_start(2, la_cur, la_slot, 0)

    def table_part():
        vside[...] = dot(pvoc[...], logits[...].astype(BF))
        ar_sum(0, sm_cur, sm_slot, 3)
        ta_cur[0] = outer_pair(vside[...], sm_cur[4, 0:RANK, :].astype(F32))

    def relay_done(s):
        total = rs_third(1, s) + cot[chained(x, y, c, s), :].astype(F32)
        zr[own_rows(4, s), :] = total.astype(BF)
        rc(
            zr.at[own_rows(4, s)], cot.at[chained(x, y, c, s)], c_send, c_recv.at[s], dev(x, y, c, (sec + 3) % 4)
        ).start()

    @pl.when(sec != 0)
    def _():
        for s in range(PARTS):
            back(s)
            rs_sibling(1, xb, s)
            if s:
                rs_first(1, xb, s - 1)
        rs_first(1, xb, PARTS - 1)
        section_grads()
        rs_second(1, xb, 0)
        rs_second(1, xb, 1)
        relay_done(0)
        rs_second(1, xb, 2)
        relay_done(1)
        relay_done(2)
        table_part()

    @pl.when(sec == 0)
    def _():
        table_part()
        embed = dot(upside[...], hgrad[...])
        for r in range(2):
            side = embed[:, r * SEQ:(r + 1) * SEQ]
            for s in range(PARTS):
                here = span(chain_start(x, y, c, s) - dp * D, SUB)
                term = dot(pdt[here, :], cot[chained(x, y, c, s), :], ((0,), (0,)))[0:RANK, :]
                side = side + jnp.where(dp == r, term, jnp.zeros_like(term))
            token = sm_cur[4, RANK:2 * RANK, r * SEQ:(r + 1) * SEQ].astype(F32)
            ta_cur[0, r * FOLD:(r + 1) * FOLD, :] += math.sqrt(D) * fold(
                dot(token, side, ((1,), (1,)), lax.Precision.HIGHEST)
            )

    pair_start(3, ta_cur, ta_slot, 0)

    @pl.when(sec == 0)
    def _():
        section_grads()

    for phase in range(3):
        pair_sum(3, ta_cur, ta_slot, phase)
        pair_start(3, ta_cur, ta_slot, phase + 1)
        pair_sum(2, la_cur, la_slot, phase)
        if phase < 2:
            pair_start(2, la_cur, la_slot, phase + 1)
    unfold(lay_out, la_cur, 3)

    ag_drain(2, cot)
    rs_drain(0, fh)
    ar_drain(0, sm_slot, 10)
    ar_drain(1, st_slot, 19)
    pair_drain(2, la_slot, 6)

    @pl.when(sec != 3)
    def _():
        rc(piece(zr, 3), piece(zr, 3), z_send, z_recv.at[0, 0], sib).wait_send()

    @pl.when(sec != 0)
    def _():
        rc(piece(zr, 4), piece(zr, 4), c_send, c_recv.at[0], sib).wait_send()
        rs_drain(1, xb)

    @pl.when(sec == 0)
    def _():
        ag_drain(3, pdt)

    pair_sum(3, ta_cur, ta_slot, 3)
    unfold(tab_out, ta_cur, 4)
    pair_drain(3, ta_slot, 9)


def shards(x_in, final_hidden, w_up, w_down, table, token_ids, targets, proj_in, proj_out, proj_vocab, proj_dim):
    vmem = pl.BlockSpec(memory_space=pltpu.VMEM)
    hbm = pl.BlockSpec(memory_space=pl.ANY)
    full = lambda n: pltpu.VMEM((n * ROWS, SEQ), BF)
    dma = pltpu.SemaphoreType.DMA
    layer, tab = pl.pallas_call(
        kernel,
        out_shape=[jax.ShapeDtypeStruct((RANK, RANK), F32)] * 2,
        in_specs=[hbm] * 5 + [vmem] * 6,
        out_specs=[vmem] * 2,
        scratch_shapes=[
            pltpu.VMEM((VROWS, D), BF),
            pltpu.VMEM((UNITS, D), BF),
            pltpu.VMEM((D, UNITS), BF),
            pltpu.VMEM((UNITS, D), BF),
            full(32), full(32), full(32), full(32),
            full(2 * 16), full(2 * 12), full(2 * 3), full(5),
            pltpu.VMEM((VROWS, TOK), F32),
            pltpu.VMEM((TOK, VROWS), BF),
            pltpu.VMEM((UNITS, TOK), F32),
            pltpu.VMEM((UNITS, TOK), F32),
            pltpu.VMEM((UNITS, TOK), BF),
            pltpu.VMEM((RANK, TOK), F32),
            pltpu.VMEM((RANK, TOK), F32),
            pltpu.VMEM((RANK, UNITS), BF),
            pltpu.VMEM((ROWS, SEQ), F32),
            pltpu.VMEM((4 * ROWS, SEQ), F32),
            pltpu.VMEM((5, 2 * RANK, TOK), BF),
            pltpu.VMEM((10, 2 * RANK, TOK), BF),
            pltpu.VMEM((4, 8, TOK), F32),
            pltpu.VMEM((19, 8, TOK), F32),
            pltpu.VMEM((5, RANK, 2 * RANK), F32),
            pltpu.VMEM((10, RANK, 2 * RANK), F32),
            pltpu.VMEM((5, RANK, 2 * RANK), F32),
            pltpu.VMEM((10, RANK, 2 * RANK), F32),
            dma((5,)),
            dma((4,)), dma((4, PARTS, 32)),
            dma((2,)), dma((2, 11 * PARTS)),
            dma(()), dma((PARTS, 3)),
            dma(()), dma((PARTS,)),
            dma((4,)), dma((4, 19)),
        ],
        compiler_params=pltpu.CompilerParams(
            collective_id=0, has_side_effects=True, vmem_limit_bytes=62 * 1024 * 1024
        ),
    )(
        x_in[0], final_hidden, jnp.swapaxes(w_up[0], 0, 1), w_down[0], table,
        token_ids.reshape(1, TOK), targets.reshape(1, TOK),
        proj_in[0], proj_out[0], proj_vocab, proj_dim,
    )
    return layer[None, None], tab[None]


def solution(mesh):
    placed = (
        P("section", "tensor", "dp"),
        P("tensor", "dp"),
        P("section", None, ("tensor", "dp")),
        P("section", ("tensor", "dp"), None),
        P(("section", "tensor", "dp"), None),
        P(),
        P(),
        P("section", None, ("tensor", "dp")),
        P("section", None, None),
        P(None, ("section", "tensor", "dp")),
        P(None, "tensor"),
    )
    return jax.shard_map(
        shards,
        mesh=mesh,
        in_specs=placed,
        out_specs=(P("section", "dp", None, None), P("dp", None, None)),
        check_vma=False,
    )
```

```python
import math

import jax
import jax.numpy as jnp
from jax import lax
from jax.experimental import pallas as pl
from jax.experimental.pallas import tpu as pltpu
from jax.sharding import PartitionSpec as P

D = 5376
TOK = 256
SEQ = 128
RANK = 64
UNITS = 672
VROWS = 1024
ROWS = 336
PARTS = 3
SUB = ROWS // PARTS
PART = D // PARTS
HALF = D // 2
FOLD = RANK // 2
TB = 384
HB = 896
BF = jnp.bfloat16
F32 = jnp.float32


def dot(a, b, dims=((1,), (0,)), precision=None):
    return lax.dot_general(a, b, (dims, ((), ())), preferred_element_type=F32, precision=precision)


def outer_pair(left, right):
    parts = [
        fold(dot(left[:, q * SEQ:(q + 1) * SEQ], right[:, q * SEQ:(q + 1) * SEQ], ((1,), (1,)), lax.Precision.HIGHEST))
        for q in range(2)
    ]
    return jnp.concatenate(parts, axis=0)


def fold(square):
    return jnp.concatenate([square[0:FOLD, :], square[FOLD:RANK, :]], axis=1)


def kernel(
    x_hbm, fh_hbm, wupt_hbm, wdn_hbm, tab_hbm, tok, tgt, pin, pout, pvoc, pdim,
    both_out,
    tab, wupt, wup, wdn, fh, xb, cot, pdt,
    r0, r1, r2, zr,
    logits, gradt, act, slope, hgrad, inproj, vside, upside, own, sums,
    sm_cur, sm_slot, st_cur, st_slot, la_cur, la_slot, ta_cur, ta_slot,
    lsem, ag_send, ag_recv, rs_send, rs_recv, z_send, z_recv, c_send, c_recv, ar_send, ar_recv,
):
    sec = lax.axis_index("section")
    ten = lax.axis_index("tensor")
    dp = lax.axis_index("dp")
    c = ten % 2
    y = (ten // 2) % 4
    lo = ten // 8
    x = dp * 2 + lo

    def dev(xx, yy, cc, zz):
        return (zz, (xx % 2) * 8 + yy * 2 + cc, xx // 2)

    def at(ka, kb):
        return (x + ka * (1 - c) + kb * c) % 4, (y + ka * c + kb * (1 - c)) % 4

    def cidx(xx, yy, cc):
        return xx * 8 + yy * 2 + cc

    def rows(i):
        return pl.ds(pl.multiple_of(i * ROWS, 16), ROWS)

    def piece(ref, i):
        return ref.at[rows(i)]

    def span(start, count):
        return pl.ds(pl.multiple_of(start, 16), count)

    def given(xx, yy, cc, s):
        return span((xx * 8 + yy * 2 + cc) * ROWS + s * SUB, SUB)

    def chain_start(xx, yy, cc, s):
        spot = (1 - cc) * ((xx % 2) * 4 + yy) + cc * (yy * 2 + xx % 2)
        return (xx // 2) * D + s * PART + (cc * 8 + spot) * SUB

    def chained(xx, yy, cc, s):
        return span(chain_start(xx, yy, cc, s), SUB)

    def rc(src, dst, ssem, rsem, device):
        return pltpu.make_async_remote_copy(
            src_ref=src, dst_ref=dst, send_sem=ssem, recv_sem=rsem,
            device_id=device, device_id_type=pl.DeviceIdType.MESH,
        )

    sib = dev(x, y, 1 - c, sec)
    mine = cidx(x, y, c)

    local = [
        pltpu.make_async_copy(fh_hbm, piece(fh, mine), lsem.at[0]),
        pltpu.make_async_copy(x_hbm, piece(xb, mine), lsem.at[1]),
        pltpu.make_async_copy(wupt_hbm, wupt, lsem.at[2]),
        pltpu.make_async_copy(tab_hbm, tab, lsem.at[3]),
        pltpu.make_async_copy(wdn_hbm, wdn, lsem.at[4]),
    ]
    for copy in local:
        copy.start()

    barrier = pltpu.get_barrier_semaphore()
    partners = [sib]
    for k in range(1, 4):
        partners.append(dev((x + k) % 4, y, c, sec))
        partners.append(dev(x, (y + k) % 4, c, sec))
        partners.append(dev(x, y, c, (sec + k) % 4))
        for j in range(1, 4):
            partners.append(dev((x + j) % 4, (y + k) % 4, c, sec))
    for partner in partners:
        pl.semaphore_signal(barrier, inc=1, device_id=partner, device_id_type=pl.DeviceIdType.MESH)
    pl.semaphore_wait(barrier, len(partners))

    def ag_copy(n, buf, where, chip, cc, s, device):
        xx, yy = chip
        ref = buf.at[where(xx, yy, cc, s)]
        return rc(ref, ref, ag_send.at[n], ag_recv.at[n, s, cidx(xx, yy, cc)], device)

    def ag_first(n, buf, where, s):
        for k in range(1, 4):
            ag_copy(n, buf, where, (x, y), c, s, dev(*at(k, 0), c, sec)).start()
        for k in range(1, 4):
            ag_copy(n, buf, where, (x, y), c, s, dev(*at(0, k), c, sec)).start()
        ag_copy(n, buf, where, (x, y), c, s, sib).start()

    def ag_second(n, buf, where, s):
        for ka in range(1, 4):
            chip = at(4 - ka, 0)
            ag_copy(n, buf, where, chip, c, s, sib).wait_recv()
            for kb in range(1, 4):
                ag_copy(n, buf, where, chip, c, s, dev(*at(0, kb), c, sec)).start()
            ag_copy(n, buf, where, chip, c, s, sib).start()

    def ag_third(n, buf, where, s):
        def body(j, carry):
            chip = at(4 - j // 3, 3 - j % 3)
            ag_copy(n, buf, where, chip, c, s, sib).wait_recv()
            ag_copy(n, buf, where, chip, c, s, sib).start()
            return carry

        lax.fori_loop(0, 12, body, 0)

    def ag_last(n, buf, where, s):
        def body(j, carry):
            ag_copy(n, buf, where, (j // 4, j % 4), 1 - c, s, sib).wait_recv()
            return carry

        lax.fori_loop(0, 16, body, 0)

    def ag_drain(n, buf):
        whole = buf.at[pl.ds(0, 31 * ROWS)]
        rc(whole, whole, ag_send.at[n], ag_recv.at[n, 0, 0], sib).wait_send()

    b_own = y * (1 - c) + x * c

    def rs_copy(n, src, ref, start, count, sem, device, src_start):
        return rc(
            src.at[span(src_start, count)], ref.at[span(start, count)], rs_send.at[n], rs_recv.at[n, sem], device
        )

    def rs_sibling(n, src, s):
        for r in range(2):
            start = ((n * PARTS + s) * 2 + r) * 8 * SUB
            rs_copy(n, src, r0, start, 8 * SUB, s * 11 + r, sib, r * D + s * PART + (1 - c) * 8 * SUB).start()

    def run_start(ka, u, s):
        aa = (x * (1 - c) + y * c + ka) % 4
        return chain_start(aa * (1 - c) + 2 * u * c, aa * c + 2 * u * (1 - c), c, s)

    def rs_first(n, src, s):
        for r in range(2):
            start = ((n * PARTS + s) * 2 + r) * 8 * SUB
            rs_copy(n, r0, r0, start, 8 * SUB, s * 11 + r, sib, start).wait_recv()
            here = span(r * D + s * PART + c * 8 * SUB, 8 * SUB)
            src[here, :] = (src[here, :].astype(F32) + r0[span(start, 8 * SUB), :].astype(F32)).astype(BF)
        for ka in (2, 1, 3):
            for u in range(2):
                start = ((n * PARTS + s) * 3 + ka - 1) * 4 * SUB + u * 2 * SUB
                rs_copy(
                    n, src, r1, start, 2 * SUB, s * 11 + 2 + (ka - 1) * 2 + u, dev(*at(ka, 0), c, sec),
                    run_start(ka, u, s),
                ).start()

    def rs_second(n, src, s):
        for u in range(2):
            here = span(run_start(0, u, s), 2 * SUB)
            total = src[here, :].astype(F32)
            for k in range(3):
                start = ((n * PARTS + s) * 3 + k) * 4 * SUB + u * 2 * SUB
                rs_copy(n, r1, r1, start, 2 * SUB, s * 11 + 2 + k * 2 + u, sib, start).wait_recv()
                total = total + r1[span(start, 2 * SUB), :].astype(F32)
            sums[pl.ds((s * 4 + u * 2) * SUB, 2 * SUB), :] = total
            src[here, :] = total.astype(BF)
        for kb in range(1, 4):
            xx, yy = at(0, kb)
            start = ((n * PARTS + s) * 3 + kb - 1) * SUB
            rs_copy(
                n, src, r2, start, SUB, s * 11 + 7 + kb, dev(xx, yy, c, sec), chain_start(xx, yy, c, s)
            ).start()

    def rs_third(n, s):
        total = sums[span((s * 4 + b_own) * SUB, SUB), :]
        for k in range(3):
            start = ((n * PARTS + s) * 3 + k) * SUB
            rs_copy(n, r2, r2, start, SUB, s * 11 + 8 + k, sib, start).wait_recv()
            total = total + r2[span(start, SUB), :].astype(F32)
        return total

    def rs_drain(n, src):
        whole = src.at[pl.ds(0, 31 * ROWS)]
        rc(whole, whole, rs_send.at[n], rs_recv.at[n, 0], sib).wait_send()

    def ar_peers(phase):
        if phase == 0:
            return [(0, sib)]
        if phase == 1:
            return [(k, dev((x + k) % 4, y, c, sec)) for k in (1, 2, 3)]
        if phase == 2:
            return [(3 + k, dev(x, (y + k) % 4, c, sec)) for k in (1, 2, 3)]
        return [(6 + k, dev(x, y, c, (sec + k) % 4)) for k in (1, 2, 3)]

    def ar_copies(n, cur, slot, phase):
        return [
            rc(cur.at[phase], slot.at[s], ar_send.at[n], ar_recv.at[n, s], device)
            for s, device in ar_peers(phase)
        ]

    def ar_start(n, cur, slot, phase):
        for copy in ar_copies(n, cur, slot, phase):
            copy.start()

    def ar_wait(n, cur, slot, phase):
        for copy in ar_copies(n, cur, slot, phase):
            copy.wait_recv()

    def ar_sum(n, cur, slot, phase):
        ar_wait(n, cur, slot, phase)
        total = cur[phase].astype(F32)
        for s, _ in ar_peers(phase):
            total = total + slot[s].astype(F32)
        cur[phase + 1] = total.astype(cur.dtype)

    def pair_copies(n, cur, slot, phase):
        copies = []
        for s, device in ar_peers(phase):
            if phase == 0:
                src, dst = cur.at[0], slot.at[0]
            elif phase == 1:
                src = cur.at[1, pl.ds(pl.multiple_of(((x + s) % 4) // 2 * FOLD, FOLD), FOLD)]
                dst = slot.at[s, pl.ds(0, FOLD)]
            else:
                src, dst = cur.at[phase, pl.ds(0, FOLD)], slot.at[s, pl.ds(0, FOLD)]
            copies.append(rc(src, dst, ar_send.at[n], ar_recv.at[n, s], device))
        return copies

    def pair_start(n, cur, slot, phase):
        for copy in pair_copies(n, cur, slot, phase):
            copy.start()

    def pair_sum(n, cur, slot, phase):
        for copy in pair_copies(n, cur, slot, phase):
            copy.wait_recv()
        if phase == 0:
            cur[1] = cur[0] + slot[0]
            return
        total = cur[1, pl.ds(pl.multiple_of(dp * FOLD, FOLD), FOLD), :] if phase == 1 else cur[phase, 0:FOLD, :]
        for s, _ in ar_peers(phase):
            total = total + slot[s, 0:FOLD, :]
        cur[phase + 1, 0:FOLD, :] = total

    def pair_drain(n, slot, count):
        part = slot.at[pl.ds(0, 1)]
        rc(part, part, ar_send.at[n], ar_recv.at[n, 0], sib).wait_send()
        part = slot.at[pl.ds(1, count), pl.ds(0, FOLD)]
        rc(part, part, ar_send.at[n], ar_recv.at[n, 0], sib).wait_send()

    def unfold(out, cur, phase):
        out[0:FOLD, :] = cur[phase, 0:FOLD, 0:RANK]
        out[FOLD:RANK, :] = cur[phase, 0:FOLD, RANK:2 * RANK]

    def ar_drain(n, slot, count):
        part = slot.at[pl.ds(0, count)]
        rc(part, part, ar_send.at[n], ar_recv.at[n, 0], sib).wait_send()

    def feature_half(buf, h):
        return jnp.concatenate([buf[pl.ds(h * HALF, HALF), :], buf[pl.ds(D + h * HALF, HALF), :]], axis=1)

    local[0].wait()
    for s in range(PARTS):
        ag_first(0, fh, given, s)
    local[1].wait()

    columns = ((sec * 16 + ten) * 2 + dp) * VROWS + lax.broadcasted_iota(jnp.int32, (VROWS, TOK), 0)
    dim_part = dot(pdim[...], fh[rows(mine), :])
    dim_part = jnp.where(sec == 0, dim_part, jnp.zeros_like(dim_part))
    blank = jnp.zeros_like(dim_part)
    sm_cur[0, 0:RANK, 0:SEQ] = jnp.where(dp == 0, dim_part, blank).astype(BF)
    sm_cur[0, 0:RANK, SEQ:TOK] = jnp.where(dp == 1, dim_part, blank).astype(BF)
    token_hot = jnp.where(tok[...] == columns, 1.0, 0.0).astype(BF)
    sm_cur[0, RANK:2 * RANK, :] = dot(pvoc[...], token_hot).astype(BF)

    pdt[rows(mine), :] = jnp.concatenate([pdim[...].T, jnp.zeros((ROWS, SEQ - RANK), BF)], axis=1)

    for s in range(PARTS):
        ag_second(0, fh, given, s)
    ar_start(0, sm_cur, sm_slot, 0)
    local[2].wait()

    def turn(b, carry):
        k0 = pl.multiple_of(b * TB, TB)
        wup[pl.ds(k0, TB), :] = wupt[:, pl.ds(k0, TB)].T
        return carry

    lax.fori_loop(0, D // TB, turn, 0)
    for s in range(PARTS):
        ag_third(0, fh, given, s)
    for s in range(PARTS):
        ag_first(1, xb, given, s)
    for s in range(PARTS):
        ag_last(0, fh, given, s)

    local[3].wait()
    logits[...] = dot(tab[:, 0:HALF], feature_half(fh, 0))
    logits[...] += dot(tab[:, HALF:D], feature_half(fh, 1))

    peak = jnp.max(logits[...], axis=0, keepdims=True)
    st_cur[0] = jnp.zeros((8, TOK), F32)
    st_cur[0, 0:1, :] = peak
    st_cur[0, 1:2, :] = jnp.sum(jnp.exp(logits[...] - peak), axis=0, keepdims=True)

    def stats_peers(phase):
        if phase == 0:
            return [(0, sib)]
        if phase == 1:
            return [
                (4 * i + j, dev((x + i) % 4, (y + j) % 4, c, sec)) for i in (2, 1, 3, 0) for j in (2, 1, 3, 0) if i or j
            ]
        return [(15 + k, dev(x, y, c, (sec + k) % 4)) for k in (2, 1, 3)]

    def stats_copies(phase):
        return [
            rc(st_cur.at[phase], st_slot.at[s], ar_send.at[1], ar_recv.at[1, s], device)
            for s, device in stats_peers(phase)
        ]

    def stats_step(phase):
        for copy in stats_copies(phase):
            copy.wait_recv()
        peaks = [st_cur[phase, 0:1, :]] + [st_slot[s, 0:1, :] for s, _ in stats_peers(phase)]
        sums = [st_cur[phase, 1:2, :]] + [st_slot[s, 1:2, :] for s, _ in stats_peers(phase)]
        top = peaks[0]
        for other in peaks[1:]:
            top = jnp.maximum(top, other)
        total = jnp.zeros_like(top)
        for a, b in zip(peaks, sums):
            total = total + b * jnp.exp(a - top)
        st_cur[phase + 1] = jnp.zeros((8, TOK), F32)
        st_cur[phase + 1, 0:1, :] = top
        st_cur[phase + 1, 1:2, :] = total
        if phase < 2:
            for copy in stats_copies(phase + 1):
                copy.start()

    for copy in stats_copies(0):
        copy.start()
    stats_step(0)
    for s in range(PARTS):
        ag_second(1, xb, given, s)
    ar_sum(0, sm_cur, sm_slot, 0)
    ar_start(0, sm_cur, sm_slot, 1)
    stats_step(1)
    ag_drain(0, fh)
    stats_step(2)

    top = st_cur[3, 0:1, :]
    scale = 1.0 / st_cur[3, 1:2, :]
    hot = jnp.where(tgt[...] == columns, 1.0, 0.0)
    grad = jnp.exp(logits[...] - top) * scale - hot
    logits[...] = grad
    gradt[...] = grad.T.astype(BF)

    def head_step(b, carry):
        k0 = pl.multiple_of(b * HB, HB)
        k1 = pl.multiple_of(D + b * HB, 16)
        block = dot(gradt[...], tab[:, pl.ds(k0, HB)]).T.astype(BF)
        fh[pl.ds(k0, HB), :] = block[:, 0:SEQ]
        fh[pl.ds(k1, HB), :] = block[:, SEQ:TOK]
        return carry

    steps = PART // HB
    for s in range(PARTS):
        lax.fori_loop(s * steps, (s + 1) * steps, head_step, 0)
        rs_sibling(0, fh, s)
        if s:
            rs_first(0, fh, s - 1)
    rs_first(0, fh, PARTS - 1)

    ar_sum(0, sm_cur, sm_slot, 1)
    ar_start(0, sm_cur, sm_slot, 2)
    for s in range(PARTS):
        ag_third(1, xb, given, s)
    for s in range(PARTS):
        ag_last(1, xb, given, s)
    hidden = dot(wupt[:, 0:HALF], feature_half(xb, 0)) + dot(wupt[:, HALF:D], feature_half(xb, 1))
    gate = jax.nn.sigmoid(hidden)
    slope[...] = gate * (1.0 + hidden * (1.0 - gate))
    inproj[...] = dot(pin[...], (hidden * gate).astype(BF))
    ar_sum(0, sm_cur, sm_slot, 2)
    ar_start(0, sm_cur, sm_slot, 3)

    def own_rows(k, s):
        return pl.ds(k * ROWS + s * SUB, SUB)

    def head_done(s):
        total = rs_third(0, s)

        @pl.when(sec == 3)
        def _():
            own[own_rows(0, s), :] = total

        @pl.when(sec != 3)
        def _():
            zr[own_rows(3, s), :] = total.astype(BF)
            rc(
                zr.at[own_rows(3, s)], zr.at[span(sec * ROWS + s * SUB, SUB)], z_send, z_recv.at[s, sec],
                dev(x, y, c, 3),
            ).start()

    def begin_last(s):
        total = own[own_rows(0, s), :]
        for z in range(3):
            held = zr.at[own_rows(z, s)]
            rc(held, held, z_send, z_recv.at[s, z], sib).wait_recv()
            total = total + zr[own_rows(z, s), :].astype(F32)
        cot[chained(x, y, c, s), :] = total.astype(BF)
        ag_first(2, cot, chained, s)

    def begin(s):
        held = cot.at[chained(x, y, c, s)]
        rc(held, held, c_send, c_recv.at[s], sib).wait_recv()
        ag_first(2, cot, chained, s)

    rs_second(0, fh, 0)
    rs_second(0, fh, 1)
    head_done(0)
    rs_second(0, fh, 2)
    head_done(1)
    local[4].wait()
    ag_drain(1, xb)

    @pl.when(sec == 3)
    def _():
        begin_last(0)

    head_done(2)

    @pl.when(sec == 3)
    def _():
        begin_last(1)
        ag_second(2, cot, chained, 0)
        begin_last(2)

    @pl.when(sec != 3)
    def _():
        @pl.when(sec == 0)
        def _():
            for s in range(PARTS):
                ag_first(3, pdt, given, s)
            for s in range(PARTS):
                ag_second(3, pdt, given, s)
            for s in range(PARTS):
                ag_third(3, pdt, given, s)
            for s in range(PARTS):
                ag_last(3, pdt, given, s)
            upside[...] = dot(wupt[...], pdt[0:D, :]).T[0:RANK, :].astype(BF)

        begin(0)
        begin(1)
        ag_second(2, cot, chained, 0)
        begin(2)

    def down(s, cc):
        k0 = pl.multiple_of(s * PART + cc * (PART // 2), 128)
        k1 = pl.multiple_of(D + s * PART + cc * (PART // 2), 16)
        right = jnp.concatenate([cot[pl.ds(k0, PART // 2), :], cot[pl.ds(k1, PART // 2), :]], axis=1)
        return dot(wdn[:, pl.ds(k0, PART // 2)], right)

    ag_second(2, cot, chained, 1)
    ag_third(2, cot, chained, 0)
    ag_second(2, cot, chained, 2)
    act[...] = down(0, c)
    ag_last(2, cot, chained, 0)
    act[...] += down(0, 1 - c)
    ag_third(2, cot, chained, 1)
    act[...] += down(1, c)
    ag_last(2, cot, chained, 1)
    act[...] += down(1, 1 - c)
    ag_third(2, cot, chained, 2)
    act[...] += down(2, c)
    ag_last(2, cot, chained, 2)
    total_act = act[...] + down(2, 1 - c)
    hgrad[...] = (total_act * slope[...]).astype(BF)

    def back(s):
        block = dot(wup[s * PART:(s + 1) * PART, :], hgrad[...]).astype(BF)
        xb[pl.ds(s * PART, PART), :] = block[:, 0:SEQ]
        xb[pl.ds(D + s * PART, PART), :] = block[:, SEQ:TOK]

    def section_grads():
        outproj = dot(pout[:, 0:HALF], feature_half(cot, 0)) + dot(pout[:, HALF:D], feature_half(cot, 1))
        la_cur[0] = outer_pair(outproj, inproj[...])
        pair_start(2, la_cur, la_slot, 0)

    def table_part():
        vside[...] = dot(pvoc[...], logits[...].astype(BF))
        ar_sum(0, sm_cur, sm_slot, 3)
        ta_cur[0] = outer_pair(vside[...], sm_cur[4, 0:RANK, :].astype(F32))

    def relay_done(s):
        total = rs_third(1, s) + cot[chained(x, y, c, s), :].astype(F32)
        zr[own_rows(4, s), :] = total.astype(BF)
        rc(
            zr.at[own_rows(4, s)], cot.at[chained(x, y, c, s)], c_send, c_recv.at[s], dev(x, y, c, (sec + 3) % 4)
        ).start()

    @pl.when(sec != 0)
    def _():
        for s in range(PARTS):
            back(s)
            rs_sibling(1, xb, s)
            if s:
                rs_first(1, xb, s - 1)
        rs_first(1, xb, PARTS - 1)
        rs_second(1, xb, 0)
        rs_second(1, xb, 1)
        relay_done(0)
        rs_second(1, xb, 2)
        relay_done(1)
        relay_done(2)
        section_grads()
        table_part()

    @pl.when(sec == 0)
    def _():
        table_part()
        embed = dot(upside[...], hgrad[...])
        for r in range(2):
            side = embed[:, r * SEQ:(r + 1) * SEQ]
            for s in range(PARTS):
                here = span(chain_start(x, y, c, s) - dp * D, SUB)
                term = dot(pdt[here, :], cot[chained(x, y, c, s), :], ((0,), (0,)))[0:RANK, :]
                side = side + jnp.where(dp == r, term, jnp.zeros_like(term))
            token = sm_cur[4, RANK:2 * RANK, r * SEQ:(r + 1) * SEQ].astype(F32)
            ta_cur[0, r * FOLD:(r + 1) * FOLD, :] += math.sqrt(D) * fold(
                dot(token, side, ((1,), (1,)), lax.Precision.HIGHEST)
            )

    pair_start(3, ta_cur, ta_slot, 0)

    @pl.when(sec == 0)
    def _():
        section_grads()

    for phase in range(3):
        pair_sum(3, ta_cur, ta_slot, phase)
        pair_start(3, ta_cur, ta_slot, phase + 1)
        pair_sum(2, la_cur, la_slot, phase)
        if phase < 2:
            pair_start(2, la_cur, la_slot, phase + 1)
    unfold(both_out.at[0], la_cur, 3)

    ag_drain(2, cot)
    rs_drain(0, fh)
    ar_drain(0, sm_slot, 10)
    ar_drain(1, st_slot, 19)
    pair_drain(2, la_slot, 6)

    @pl.when(sec != 3)
    def _():
        rc(piece(zr, 3), piece(zr, 3), z_send, z_recv.at[0, 0], sib).wait_send()

    @pl.when(sec != 0)
    def _():
        rc(piece(zr, 4), piece(zr, 4), c_send, c_recv.at[0], sib).wait_send()
        rs_drain(1, xb)

    @pl.when(sec == 0)
    def _():
        ag_drain(3, pdt)

    pair_sum(3, ta_cur, ta_slot, 3)
    unfold(both_out.at[1], ta_cur, 4)
    pair_drain(3, ta_slot, 9)


def shards(x_in, final_hidden, w_up, w_down, table, token_ids, targets, proj_in, proj_out, proj_vocab, proj_dim):
    vmem = pl.BlockSpec(memory_space=pltpu.VMEM)
    hbm = pl.BlockSpec(memory_space=pl.ANY)
    full = lambda n: pltpu.VMEM((n * ROWS, SEQ), BF)
    dma = pltpu.SemaphoreType.DMA
    both = pl.pallas_call(
        kernel,
        out_shape=jax.ShapeDtypeStruct((2, RANK, RANK), F32),
        in_specs=[hbm] * 5 + [vmem] * 6,
        out_specs=vmem,
        scratch_shapes=[
            pltpu.VMEM((VROWS, D), BF),
            pltpu.VMEM((UNITS, D), BF),
            pltpu.VMEM((D, UNITS), BF),
            pltpu.VMEM((UNITS, D), BF),
            full(32), full(32), full(32), full(32),
            full(2 * 16), full(2 * 12), full(2 * 3), full(5),
            pltpu.VMEM((VROWS, TOK), F32),
            pltpu.VMEM((TOK, VROWS), BF),
            pltpu.VMEM((UNITS, TOK), F32),
            pltpu.VMEM((UNITS, TOK), F32),
            pltpu.VMEM((UNITS, TOK), BF),
            pltpu.VMEM((RANK, TOK), F32),
            pltpu.VMEM((RANK, TOK), F32),
            pltpu.VMEM((RANK, UNITS), BF),
            pltpu.VMEM((ROWS, SEQ), F32),
            pltpu.VMEM((4 * ROWS, SEQ), F32),
            pltpu.VMEM((5, 2 * RANK, TOK), BF),
            pltpu.VMEM((10, 2 * RANK, TOK), BF),
            pltpu.VMEM((4, 8, TOK), F32),
            pltpu.VMEM((19, 8, TOK), F32),
            pltpu.VMEM((5, RANK, 2 * RANK), F32),
            pltpu.VMEM((10, RANK, 2 * RANK), F32),
            pltpu.VMEM((5, RANK, 2 * RANK), F32),
            pltpu.VMEM((10, RANK, 2 * RANK), F32),
            dma((5,)),
            dma((4,)), dma((4, PARTS, 32)),
            dma((2,)), dma((2, 11 * PARTS)),
            dma(()), dma((PARTS, 3)),
            dma(()), dma((PARTS,)),
            dma((4,)), dma((4, 19)),
        ],
        compiler_params=pltpu.CompilerParams(
            collective_id=0, has_side_effects=True, vmem_limit_bytes=62 * 1024 * 1024
        ),
    )(
        x_in[0], final_hidden, jnp.swapaxes(w_up[0], 0, 1), w_down[0], table,
        token_ids.reshape(1, TOK), targets.reshape(1, TOK),
        proj_in[0], proj_out[0], proj_vocab, proj_dim,
    )
    return both[0][None, None], both[1][None]


def solution(mesh):
    placed = (
        P("section", "tensor", "dp"),
        P("tensor", "dp"),
        P("section", None, ("tensor", "dp")),
        P("section", ("tensor", "dp"), None),
        P(("section", "tensor", "dp"), None),
        P(),
        P(),
        P("section", None, ("tensor", "dp")),
        P("section", None, None),
        P(None, ("section", "tensor", "dp")),
        P(None, "tensor"),
    )
    return jax.shard_map(
        shards,
        mesh=mesh,
        in_specs=placed,
        out_specs=(P("section", "dp", None, None), P("dp", None, None)),
        check_vma=False,
    )
```

```python
import math

import jax
import jax.numpy as jnp
from jax import lax
from jax.experimental import pallas as pl
from jax.experimental.pallas import tpu as pltpu
from jax.sharding import PartitionSpec as P

D = 5376
TOK = 256
SEQ = 128
RANK = 64
UNITS = 672
VROWS = 1024
ROWS = 336
PARTS = 3
SUB = ROWS // PARTS
PART = D // PARTS
HALF = D // 2
FOLD = RANK // 2
TB = 384
HB = 896
BF = jnp.bfloat16
F32 = jnp.float32


def dot(a, b, dims=((1,), (0,)), precision=None):
    return lax.dot_general(a, b, (dims, ((), ())), preferred_element_type=F32, precision=precision)


def outer_pair(left, right):
    parts = [
        fold(dot(left[:, q * SEQ:(q + 1) * SEQ], right[:, q * SEQ:(q + 1) * SEQ], ((1,), (1,)), lax.Precision.HIGHEST))
        for q in range(2)
    ]
    return jnp.concatenate(parts, axis=0)


def fold(square):
    return jnp.concatenate([square[0:FOLD, :], square[FOLD:RANK, :]], axis=1)


def kernel(
    x_hbm, fh_hbm, wupt_hbm, wdn_hbm, tab_hbm, tok, tgt, pin, pout, pvoc, pdim,
    both_out,
    tab, wupt, wup, wdn, fh, xb, cot, pdt,
    r0, r1, r2, zr,
    logits, gradt, act, slope, hgrad, inproj, vside, upside, own, sums,
    sm_cur, sm_slot, st_cur, st_slot, la_cur, la_slot, ta_cur, ta_slot,
    lsem, ag_send, ag_recv, rs_send, rs_recv, z_send, z_recv, c_send, c_recv, ar_send, ar_recv,
):
    sec = lax.axis_index("section")
    ten = lax.axis_index("tensor")
    dp = lax.axis_index("dp")
    c = ten % 2
    y = (ten // 2) % 4
    lo = ten // 8
    x = dp * 2 + lo

    def dev(xx, yy, cc, zz):
        return (zz, (xx % 2) * 8 + yy * 2 + cc, xx // 2)

    def at(ka, kb):
        return (x + ka * (1 - c) + kb * c) % 4, (y + ka * c + kb * (1 - c)) % 4

    def cidx(xx, yy, cc):
        return xx * 8 + yy * 2 + cc

    def rows(i):
        return pl.ds(pl.multiple_of(i * ROWS, 16), ROWS)

    def piece(ref, i):
        return ref.at[rows(i)]

    def span(start, count):
        return pl.ds(pl.multiple_of(start, 16), count)

    def given(xx, yy, cc, s):
        return span((xx * 8 + yy * 2 + cc) * ROWS + s * SUB, SUB)

    def chain_start(xx, yy, cc, s):
        spot = (1 - cc) * ((xx % 2) * 4 + yy) + cc * (yy * 2 + xx % 2)
        return (xx // 2) * D + s * PART + (cc * 8 + spot) * SUB

    def chained(xx, yy, cc, s):
        return span(chain_start(xx, yy, cc, s), SUB)

    def rc(src, dst, ssem, rsem, device):
        return pltpu.make_async_remote_copy(
            src_ref=src, dst_ref=dst, send_sem=ssem, recv_sem=rsem,
            device_id=device, device_id_type=pl.DeviceIdType.MESH,
        )

    sib = dev(x, y, 1 - c, sec)
    mine = cidx(x, y, c)

    local = [
        pltpu.make_async_copy(fh_hbm, piece(fh, mine), lsem.at[0]),
        pltpu.make_async_copy(x_hbm, piece(xb, mine), lsem.at[1]),
        pltpu.make_async_copy(wupt_hbm, wupt, lsem.at[2]),
        pltpu.make_async_copy(tab_hbm, tab, lsem.at[3]),
        pltpu.make_async_copy(wdn_hbm, wdn, lsem.at[4]),
    ]
    for copy in local:
        copy.start()

    barrier = pltpu.get_barrier_semaphore()
    partners = [sib]
    for k in range(1, 4):
        partners.append(dev((x + k) % 4, y, c, sec))
        partners.append(dev(x, (y + k) % 4, c, sec))
        partners.append(dev(x, y, c, (sec + k) % 4))
        for j in range(1, 4):
            partners.append(dev((x + j) % 4, (y + k) % 4, c, sec))
    for partner in partners:
        pl.semaphore_signal(barrier, inc=1, device_id=partner, device_id_type=pl.DeviceIdType.MESH)
    pl.semaphore_wait(barrier, len(partners))

    def ag_copy(n, buf, where, chip, cc, s, device):
        xx, yy = chip
        ref = buf.at[where(xx, yy, cc, s)]
        return rc(ref, ref, ag_send.at[n], ag_recv.at[n, s, cidx(xx, yy, cc)], device)

    def ag_first(n, buf, where, s):
        for k in range(1, 4):
            ag_copy(n, buf, where, (x, y), c, s, dev(*at(k, 0), c, sec)).start()
        for k in range(1, 4):
            ag_copy(n, buf, where, (x, y), c, s, dev(*at(0, k), c, sec)).start()
        ag_copy(n, buf, where, (x, y), c, s, sib).start()

    def ag_second(n, buf, where, s):
        for ka in range(1, 4):
            chip = at(4 - ka, 0)
            ag_copy(n, buf, where, chip, c, s, sib).wait_recv()
            for kb in range(1, 4):
                ag_copy(n, buf, where, chip, c, s, dev(*at(0, kb), c, sec)).start()
            ag_copy(n, buf, where, chip, c, s, sib).start()

    def ag_third(n, buf, where, s):
        def body(j, carry):
            chip = at(4 - j // 3, 3 - j % 3)
            ag_copy(n, buf, where, chip, c, s, sib).wait_recv()
            ag_copy(n, buf, where, chip, c, s, sib).start()
            return carry

        lax.fori_loop(0, 12, body, 0)

    def ag_last(n, buf, where, s):
        def body(j, carry):
            ag_copy(n, buf, where, (j // 4, j % 4), 1 - c, s, sib).wait_recv()
            return carry

        lax.fori_loop(0, 16, body, 0)

    def ag_drain(n, buf):
        whole = buf.at[pl.ds(0, 31 * ROWS)]
        rc(whole, whole, ag_send.at[n], ag_recv.at[n, 0, 0], sib).wait_send()

    b_own = y * (1 - c) + x * c

    def rs_copy(n, src, ref, start, count, sem, device, src_start):
        return rc(
            src.at[span(src_start, count)], ref.at[span(start, count)], rs_send.at[n], rs_recv.at[n, sem], device
        )

    def rs_sibling(n, src, s):
        for r in range(2):
            start = ((n * PARTS + s) * 2 + r) * 8 * SUB
            rs_copy(n, src, r0, start, 8 * SUB, s * 11 + r, sib, r * D + s * PART + (1 - c) * 8 * SUB).start()

    def run_start(ka, u, s):
        aa = (x * (1 - c) + y * c + ka) % 4
        return chain_start(aa * (1 - c) + 2 * u * c, aa * c + 2 * u * (1 - c), c, s)

    def rs_first(n, src, s):
        for r in range(2):
            start = ((n * PARTS + s) * 2 + r) * 8 * SUB
            rs_copy(n, r0, r0, start, 8 * SUB, s * 11 + r, sib, start).wait_recv()
            here = span(r * D + s * PART + c * 8 * SUB, 8 * SUB)
            src[here, :] = (src[here, :].astype(F32) + r0[span(start, 8 * SUB), :].astype(F32)).astype(BF)
        for ka in (2, 1, 3):
            for u in range(2):
                start = ((n * PARTS + s) * 3 + ka - 1) * 4 * SUB + u * 2 * SUB
                rs_copy(
                    n, src, r1, start, 2 * SUB, s * 11 + 2 + (ka - 1) * 2 + u, dev(*at(ka, 0), c, sec),
                    run_start(ka, u, s),
                ).start()

    def rs_second(n, src, s):
        for u in range(2):
            here = span(run_start(0, u, s), 2 * SUB)
            total = src[here, :].astype(F32)
            for k in range(3):
                start = ((n * PARTS + s) * 3 + k) * 4 * SUB + u * 2 * SUB
                rs_copy(n, r1, r1, start, 2 * SUB, s * 11 + 2 + k * 2 + u, sib, start).wait_recv()
                total = total + r1[span(start, 2 * SUB), :].astype(F32)
            sums[pl.ds((s * 4 + u * 2) * SUB, 2 * SUB), :] = total
            src[here, :] = total.astype(BF)
        for kb in range(1, 4):
            xx, yy = at(0, kb)
            start = ((n * PARTS + s) * 3 + kb - 1) * SUB
            rs_copy(
                n, src, r2, start, SUB, s * 11 + 7 + kb, dev(xx, yy, c, sec), chain_start(xx, yy, c, s)
            ).start()

    def rs_third(n, s):
        total = sums[span((s * 4 + b_own) * SUB, SUB), :]
        for k in range(3):
            start = ((n * PARTS + s) * 3 + k) * SUB
            rs_copy(n, r2, r2, start, SUB, s * 11 + 8 + k, sib, start).wait_recv()
            total = total + r2[span(start, SUB), :].astype(F32)
        return total

    def rs_drain(n, src):
        whole = src.at[pl.ds(0, 31 * ROWS)]
        rc(whole, whole, rs_send.at[n], rs_recv.at[n, 0], sib).wait_send()

    def ar_peers(phase):
        if phase == 0:
            return [(0, sib)]
        if phase == 1:
            return [(k, dev((x + k) % 4, y, c, sec)) for k in (1, 2, 3)]
        if phase == 2:
            return [(3 + k, dev(x, (y + k) % 4, c, sec)) for k in (1, 2, 3)]
        return [(6 + k, dev(x, y, c, (sec + k) % 4)) for k in (1, 2, 3)]

    def ar_copies(n, cur, slot, phase):
        return [
            rc(cur.at[phase], slot.at[s], ar_send.at[n], ar_recv.at[n, s], device)
            for s, device in ar_peers(phase)
        ]

    def ar_start(n, cur, slot, phase):
        for copy in ar_copies(n, cur, slot, phase):
            copy.start()

    def ar_wait(n, cur, slot, phase):
        for copy in ar_copies(n, cur, slot, phase):
            copy.wait_recv()

    def ar_sum(n, cur, slot, phase):
        ar_wait(n, cur, slot, phase)
        total = cur[phase].astype(F32)
        for s, _ in ar_peers(phase):
            total = total + slot[s].astype(F32)
        cur[phase + 1] = total.astype(cur.dtype)

    def pair_copies(n, cur, slot, phase):
        copies = []
        for s, device in ar_peers(phase):
            if phase == 0:
                src, dst = cur.at[0], slot.at[0]
            elif phase == 1:
                src = cur.at[1, pl.ds(pl.multiple_of(((x + s) % 4) // 2 * FOLD, FOLD), FOLD)]
                dst = slot.at[s, pl.ds(0, FOLD)]
            else:
                src, dst = cur.at[phase, pl.ds(0, FOLD)], slot.at[s, pl.ds(0, FOLD)]
            copies.append(rc(src, dst, ar_send.at[n], ar_recv.at[n, s], device))
        return copies

    def pair_start(n, cur, slot, phase):
        for copy in pair_copies(n, cur, slot, phase):
            copy.start()

    def pair_sum(n, cur, slot, phase):
        for copy in pair_copies(n, cur, slot, phase):
            copy.wait_recv()
        if phase == 0:
            cur[1] = cur[0] + slot[0]
            return
        total = cur[1, pl.ds(pl.multiple_of(dp * FOLD, FOLD), FOLD), :] if phase == 1 else cur[phase, 0:FOLD, :]
        for s, _ in ar_peers(phase):
            total = total + slot[s, 0:FOLD, :]
        cur[phase + 1, 0:FOLD, :] = total

    def pair_drain(n, slot, count):
        part = slot.at[pl.ds(0, 1)]
        rc(part, part, ar_send.at[n], ar_recv.at[n, 0], sib).wait_send()
        part = slot.at[pl.ds(1, count), pl.ds(0, FOLD)]
        rc(part, part, ar_send.at[n], ar_recv.at[n, 0], sib).wait_send()

    def unfold(out, cur, phase):
        out[0:FOLD, :] = cur[phase, 0:FOLD, 0:RANK]
        out[FOLD:RANK, :] = cur[phase, 0:FOLD, RANK:2 * RANK]

    def ar_drain(n, slot, count):
        part = slot.at[pl.ds(0, count)]
        rc(part, part, ar_send.at[n], ar_recv.at[n, 0], sib).wait_send()

    def feature_half(buf, h):
        return jnp.concatenate([buf[pl.ds(h * HALF, HALF), :], buf[pl.ds(D + h * HALF, HALF), :]], axis=1)

    local[0].wait()
    for s in range(PARTS):
        ag_first(0, fh, given, s)
    local[1].wait()

    columns = ((sec * 16 + ten) * 2 + dp) * VROWS + lax.broadcasted_iota(jnp.int32, (VROWS, TOK), 0)
    dim_part = dot(pdim[...], fh[rows(mine), :])
    dim_part = jnp.where(sec == 0, dim_part, jnp.zeros_like(dim_part))
    blank = jnp.zeros_like(dim_part)
    sm_cur[0, 0:RANK, 0:SEQ] = jnp.where(dp == 0, dim_part, blank).astype(BF)
    sm_cur[0, 0:RANK, SEQ:TOK] = jnp.where(dp == 1, dim_part, blank).astype(BF)
    token_hot = jnp.where(tok[...] == columns, 1.0, 0.0).astype(BF)
    sm_cur[0, RANK:2 * RANK, :] = dot(pvoc[...], token_hot).astype(BF)

    pdt[rows(mine), :] = jnp.concatenate([pdim[...].T, jnp.zeros((ROWS, SEQ - RANK), BF)], axis=1)

    for s in range(PARTS):
        ag_second(0, fh, given, s)
    ar_start(0, sm_cur, sm_slot, 0)
    local[2].wait()

    def turn(b, carry):
        k0 = pl.multiple_of(b * TB, TB)
        wup[pl.ds(k0, TB), :] = wupt[:, pl.ds(k0, TB)].T
        return carry

    lax.fori_loop(0, D // TB, turn, 0)
    for s in range(PARTS):
        ag_third(0, fh, given, s)
    for s in range(PARTS):
        ag_first(1, xb, given, s)
    for s in range(PARTS):
        ag_last(0, fh, given, s)

    local[3].wait()
    logits[...] = dot(tab[:, 0:HALF], feature_half(fh, 0))
    logits[...] += dot(tab[:, HALF:D], feature_half(fh, 1))

    peak = jnp.max(logits[...], axis=0, keepdims=True)
    st_cur[0] = jnp.zeros((8, TOK), F32)
    st_cur[0, 0:1, :] = peak
    st_cur[0, 1:2, :] = jnp.sum(jnp.exp(logits[...] - peak), axis=0, keepdims=True)

    def stats_peers(phase):
        if phase == 0:
            return [(0, sib)]
        if phase == 1:
            return [
                (4 * i + j, dev((x + i) % 4, (y + j) % 4, c, sec)) for i in (2, 1, 3, 0) for j in (2, 1, 3, 0) if i or j
            ]
        return [(15 + k, dev(x, y, c, (sec + k) % 4)) for k in (2, 1, 3)]

    def stats_copies(phase):
        return [
            rc(st_cur.at[phase], st_slot.at[s], ar_send.at[1], ar_recv.at[1, s], device)
            for s, device in stats_peers(phase)
        ]

    def stats_step(phase):
        for copy in stats_copies(phase):
            copy.wait_recv()
        peaks = [st_cur[phase, 0:1, :]] + [st_slot[s, 0:1, :] for s, _ in stats_peers(phase)]
        sums = [st_cur[phase, 1:2, :]] + [st_slot[s, 1:2, :] for s, _ in stats_peers(phase)]
        top = peaks[0]
        for other in peaks[1:]:
            top = jnp.maximum(top, other)
        total = jnp.zeros_like(top)
        for a, b in zip(peaks, sums):
            total = total + b * jnp.exp(a - top)
        st_cur[phase + 1] = jnp.zeros((8, TOK), F32)
        st_cur[phase + 1, 0:1, :] = top
        st_cur[phase + 1, 1:2, :] = total
        if phase < 2:
            for copy in stats_copies(phase + 1):
                copy.start()

    for copy in stats_copies(0):
        copy.start()
    stats_step(0)
    for s in range(PARTS):
        ag_second(1, xb, given, s)
    ar_sum(0, sm_cur, sm_slot, 0)
    ar_start(0, sm_cur, sm_slot, 1)
    stats_step(1)
    ag_drain(0, fh)
    stats_step(2)

    top = st_cur[3, 0:1, :]
    scale = 1.0 / st_cur[3, 1:2, :]
    hot = jnp.where(tgt[...] == columns, 1.0, 0.0)
    grad = jnp.exp(logits[...] - top) * scale - hot
    logits[...] = grad
    gradt[...] = grad.T.astype(BF)

    def head_step(b, carry):
        k0 = pl.multiple_of(b * HB, HB)
        k1 = pl.multiple_of(D + b * HB, 16)
        block = dot(gradt[...], tab[:, pl.ds(k0, HB)]).T.astype(BF)
        fh[pl.ds(k0, HB), :] = block[:, 0:SEQ]
        fh[pl.ds(k1, HB), :] = block[:, SEQ:TOK]
        return carry

    steps = PART // HB
    for s in range(PARTS):
        lax.fori_loop(s * steps, (s + 1) * steps, head_step, 0)
        rs_sibling(0, fh, s)
        if s:
            rs_first(0, fh, s - 1)
    rs_first(0, fh, PARTS - 1)

    ar_sum(0, sm_cur, sm_slot, 1)
    ar_start(0, sm_cur, sm_slot, 2)
    for s in range(PARTS):
        ag_third(1, xb, given, s)
    for s in range(PARTS):
        ag_last(1, xb, given, s)
    hidden = dot(wupt[:, 0:HALF], feature_half(xb, 0)) + dot(wupt[:, HALF:D], feature_half(xb, 1))
    gate = jax.nn.sigmoid(hidden)
    slope[...] = gate * (1.0 + hidden * (1.0 - gate))
    inproj[...] = dot(pin[...], (hidden * gate).astype(BF))
    ar_sum(0, sm_cur, sm_slot, 2)
    ar_start(0, sm_cur, sm_slot, 3)

    def own_rows(k, s):
        return pl.ds(k * ROWS + s * SUB, SUB)

    def head_done(s):
        total = rs_third(0, s)

        @pl.when(sec == 3)
        def _():
            own[own_rows(0, s), :] = total

        @pl.when(sec != 3)
        def _():
            zr[own_rows(3, s), :] = total.astype(BF)
            rc(
                zr.at[own_rows(3, s)], zr.at[span(sec * ROWS + s * SUB, SUB)], z_send, z_recv.at[s, sec],
                dev(x, y, c, 3),
            ).start()

    def begin_last(s):
        total = own[own_rows(0, s), :]
        for z in range(3):
            held = zr.at[own_rows(z, s)]
            rc(held, held, z_send, z_recv.at[s, z], sib).wait_recv()
            total = total + zr[own_rows(z, s), :].astype(F32)
        cot[chained(x, y, c, s), :] = total.astype(BF)
        ag_first(2, cot, chained, s)

    def begin(s):
        held = cot.at[chained(x, y, c, s)]
        rc(held, held, c_send, c_recv.at[s], sib).wait_recv()
        ag_first(2, cot, chained, s)

    def table_part():
        vside[...] = dot(pvoc[...], logits[...].astype(BF))
        ar_sum(0, sm_cur, sm_slot, 3)
        ta_cur[0] = outer_pair(vside[...], sm_cur[4, 0:RANK, :].astype(F32))

    rs_second(0, fh, 0)
    rs_second(0, fh, 1)
    head_done(0)
    rs_second(0, fh, 2)
    head_done(1)
    local[4].wait()
    ag_drain(1, xb)

    @pl.when(sec == 3)
    def _():
        begin_last(0)

    head_done(2)

    @pl.when(sec == 3)
    def _():
        begin_last(1)
        ag_second(2, cot, chained, 0)
        begin_last(2)

    @pl.when(sec != 3)
    def _():
        @pl.when(sec == 0)
        def _():
            for s in range(PARTS):
                ag_first(3, pdt, given, s)
            for s in range(PARTS):
                ag_second(3, pdt, given, s)
            for s in range(PARTS):
                ag_third(3, pdt, given, s)
            for s in range(PARTS):
                ag_last(3, pdt, given, s)
            upside[...] = dot(wupt[...], pdt[0:D, :]).T[0:RANK, :].astype(BF)
            table_part()

        begin(0)
        begin(1)
        ag_second(2, cot, chained, 0)
        begin(2)

    def down(s, cc):
        k0 = pl.multiple_of(s * PART + cc * (PART // 2), 128)
        k1 = pl.multiple_of(D + s * PART + cc * (PART // 2), 16)
        right = jnp.concatenate([cot[pl.ds(k0, PART // 2), :], cot[pl.ds(k1, PART // 2), :]], axis=1)
        return dot(wdn[:, pl.ds(k0, PART // 2)], right)

    ag_second(2, cot, chained, 1)
    ag_third(2, cot, chained, 0)
    ag_second(2, cot, chained, 2)
    act[...] = down(0, c)
    ag_last(2, cot, chained, 0)
    act[...] += down(0, 1 - c)
    ag_third(2, cot, chained, 1)
    act[...] += down(1, c)
    ag_last(2, cot, chained, 1)
    act[...] += down(1, 1 - c)
    ag_third(2, cot, chained, 2)
    act[...] += down(2, c)
    ag_last(2, cot, chained, 2)
    total_act = act[...] + down(2, 1 - c)
    hgrad[...] = (total_act * slope[...]).astype(BF)

    def back(s):
        block = dot(wup[s * PART:(s + 1) * PART, :], hgrad[...]).astype(BF)
        xb[pl.ds(s * PART, PART), :] = block[:, 0:SEQ]
        xb[pl.ds(D + s * PART, PART), :] = block[:, SEQ:TOK]

    def section_grads():
        outproj = dot(pout[:, 0:HALF], feature_half(cot, 0)) + dot(pout[:, HALF:D], feature_half(cot, 1))
        la_cur[0] = outer_pair(outproj, inproj[...])
        pair_start(2, la_cur, la_slot, 0)

    def relay_done(s):
        total = rs_third(1, s) + cot[chained(x, y, c, s), :].astype(F32)
        zr[own_rows(4, s), :] = total.astype(BF)
        rc(
            zr.at[own_rows(4, s)], cot.at[chained(x, y, c, s)], c_send, c_recv.at[s], dev(x, y, c, (sec + 3) % 4)
        ).start()

    @pl.when(sec != 0)
    def _():
        for s in range(PARTS):
            back(s)
            rs_sibling(1, xb, s)
            if s:
                rs_first(1, xb, s - 1)
        rs_first(1, xb, PARTS - 1)
        rs_second(1, xb, 0)
        rs_second(1, xb, 1)
        relay_done(0)
        rs_second(1, xb, 2)
        relay_done(1)
        relay_done(2)
        section_grads()
        table_part()

    @pl.when(sec == 0)
    def _():
        embed = dot(upside[...], hgrad[...])
        term = jnp.zeros((RANK, SEQ), F32)
        for s in range(PARTS):
            here = span(chain_start(x, y, c, s) - dp * D, SUB)
            term = term + dot(pdt[here, :], cot[chained(x, y, c, s), :], ((0,), (0,)))[0:RANK, :]
        for r in range(2):
            side = embed[:, r * SEQ:(r + 1) * SEQ] + jnp.where(dp == r, term, jnp.zeros_like(term))
            token = sm_cur[4, RANK:2 * RANK, r * SEQ:(r + 1) * SEQ].astype(F32)
            ta_cur[0, r * FOLD:(r + 1) * FOLD, :] += math.sqrt(D) * fold(
                dot(token, side, ((1,), (1,)), lax.Precision.HIGHEST)
            )

    pair_start(3, ta_cur, ta_slot, 0)

    pair_sum(3, ta_cur, ta_slot, 0)
    pair_start(3, ta_cur, ta_slot, 1)

    @pl.when(sec == 0)
    def _():
        section_grads()

    for phase in range(3):
        if phase:
            pair_sum(3, ta_cur, ta_slot, phase)
            pair_start(3, ta_cur, ta_slot, phase + 1)
        pair_sum(2, la_cur, la_slot, phase)
        if phase < 2:
            pair_start(2, la_cur, la_slot, phase + 1)
    unfold(both_out.at[0], la_cur, 3)

    ag_drain(2, cot)
    rs_drain(0, fh)
    ar_drain(0, sm_slot, 10)
    ar_drain(1, st_slot, 19)
    pair_drain(2, la_slot, 6)

    @pl.when(sec != 3)
    def _():
        rc(piece(zr, 3), piece(zr, 3), z_send, z_recv.at[0, 0], sib).wait_send()

    @pl.when(sec != 0)
    def _():
        rc(piece(zr, 4), piece(zr, 4), c_send, c_recv.at[0], sib).wait_send()
        rs_drain(1, xb)

    @pl.when(sec == 0)
    def _():
        ag_drain(3, pdt)

    pair_sum(3, ta_cur, ta_slot, 3)
    unfold(both_out.at[1], ta_cur, 4)
    pair_drain(3, ta_slot, 9)


def shards(x_in, final_hidden, w_up, w_down, table, token_ids, targets, proj_in, proj_out, proj_vocab, proj_dim):
    vmem = pl.BlockSpec(memory_space=pltpu.VMEM)
    hbm = pl.BlockSpec(memory_space=pl.ANY)
    full = lambda n: pltpu.VMEM((n * ROWS, SEQ), BF)
    dma = pltpu.SemaphoreType.DMA
    both = pl.pallas_call(
        kernel,
        out_shape=jax.ShapeDtypeStruct((2, RANK, RANK), F32),
        in_specs=[hbm] * 5 + [vmem] * 6,
        out_specs=vmem,
        scratch_shapes=[
            pltpu.VMEM((VROWS, D), BF),
            pltpu.VMEM((UNITS, D), BF),
            pltpu.VMEM((D, UNITS), BF),
            pltpu.VMEM((UNITS, D), BF),
            full(32), full(32), full(32), full(32),
            full(2 * 16), full(2 * 12), full(2 * 3), full(5),
            pltpu.VMEM((VROWS, TOK), F32),
            pltpu.VMEM((TOK, VROWS), BF),
            pltpu.VMEM((UNITS, TOK), F32),
            pltpu.VMEM((UNITS, TOK), F32),
            pltpu.VMEM((UNITS, TOK), BF),
            pltpu.VMEM((RANK, TOK), F32),
            pltpu.VMEM((RANK, TOK), F32),
            pltpu.VMEM((RANK, UNITS), BF),
            pltpu.VMEM((ROWS, SEQ), F32),
            pltpu.VMEM((4 * ROWS, SEQ), F32),
            pltpu.VMEM((5, 2 * RANK, TOK), BF),
            pltpu.VMEM((10, 2 * RANK, TOK), BF),
            pltpu.VMEM((4, 8, TOK), F32),
            pltpu.VMEM((19, 8, TOK), F32),
            pltpu.VMEM((5, RANK, 2 * RANK), F32),
            pltpu.VMEM((10, RANK, 2 * RANK), F32),
            pltpu.VMEM((5, RANK, 2 * RANK), F32),
            pltpu.VMEM((10, RANK, 2 * RANK), F32),
            dma((5,)),
            dma((4,)), dma((4, PARTS, 32)),
            dma((2,)), dma((2, 11 * PARTS)),
            dma(()), dma((PARTS, 3)),
            dma(()), dma((PARTS,)),
            dma((4,)), dma((4, 19)),
        ],
        compiler_params=pltpu.CompilerParams(
            collective_id=0, has_side_effects=True, vmem_limit_bytes=62 * 1024 * 1024
        ),
    )(
        x_in[0], final_hidden, jnp.swapaxes(w_up[0], 0, 1), w_down[0], table,
        token_ids.reshape(1, TOK), targets.reshape(1, TOK),
        proj_in[0], proj_out[0], proj_vocab, proj_dim,
    )
    return both[0][None, None], both[1][None]


def solution(mesh):
    placed = (
        P("section", "tensor", "dp"),
        P("tensor", "dp"),
        P("section", None, ("tensor", "dp")),
        P("section", ("tensor", "dp"), None),
        P(("section", "tensor", "dp"), None),
        P(),
        P(),
        P("section", None, ("tensor", "dp")),
        P("section", None, None),
        P(None, ("section", "tensor", "dp")),
        P(None, "tensor"),
    )
    return jax.shard_map(
        shards,
        mesh=mesh,
        in_specs=placed,
        out_specs=(P("section", "dp", None, None), P("dp", None, None)),
        check_vma=False,
    )
```
